512 devices in a mesh: tm: 16 (over x, z_lo), space: 32 (over y, z_hi, core).
Axes of the slice: x: 4, y: 4, z: 16 (z_hi: 4, z_lo: 4; z = z_hi * 4 + z_lo), core: 2. Of those that a mesh axis runs over, the one named last changes fastest.
Arguments:
- positions: float32 [16, 3, 3, 8192], P('tm', None, None, 'space'), may hold values from -4 to 4
- velocities: float32 [16, 3, 3, 8192], P('tm', None, None, 'space'), may hold values from -3 to 3
- masses: float32 [8192], P('space'), may hold values from 0.2 to 2
- initial_places: float32 [3, 8192], P(None, 'space'), may hold values from -4 to 4
- initial_speeds: float32 [3, 8192], P(None, 'space'), may hold values from -3 to 3
Outputs:
- node_places: float32 [16, 2, 3, 8192], P('tm', None, None, 'space')
- node_speeds: float32 [16, 2, 3, 8192], P('tm', None, None, 'space')
- end_force: float32 [16, 3, 8192], P('tm', None, 'space')
- start_places: float32 [16, 3, 8192], P('tm', None, 'space')
- start_speeds: float32 [16, 3, 8192], P('tm', None, 'space')
The draws below stay inside these ranges and needn't reach their ends.
All inputs are finite; a program needn't handle non-finite values.
Results may differ from the reference program's by a relative error of at most 0.0003.
Values sent between devices are 32-bit elements; how exact they have to be, the bound alone decides.
No kernel may reach another device: no remote copies, remote signals or barrier semaphores. Data moves between devices by JAX's collectives and lax.ppermute only.
A program may use at most 64 MiB of HBM per device.

```python
import math
import jax
import jax.numpy as jnp
from jax import lax

NODES = 3
BODIES = 8192
SLICES = 16


def shard_levels(rng, extent, split, low, largest):
    level = 1.0
    for position, blocks in split:
        heights = jax.random.uniform(jax.random.fold_in(jax.random.fold_in(rng, 6), position), (blocks,), jnp.float32, low / len(split), largest / len(split))
        level = level * jnp.repeat(jnp.exp(heights), extent[position] // blocks).reshape((-1,) + (1,) * (len(extent) - 1 - position))
    return level


def gaussian(own_key, extent, width, limit, split=(), held_as=jnp.bfloat16):
    entries = jax.random.normal(own_key, extent, jnp.float32) * width
    if len(split) > 0:
        entries = shard_levels(own_key, extent, split, -0.22, 0.18) * entries
    return jnp.clip(entries, min=-limit, max=limit).astype(held_as)


def setup_inputs(seed: int = 0) -> dict:
    key_of = jax.random.split(jax.random.key(seed), 6)
    positions = gaussian(key_of[0], (SLICES, NODES, 3, BODIES), 1.0, 4.0, ((0, 16), (3, 32)), jnp.float32)
    velocities = gaussian(key_of[1], (SLICES, NODES, 3, BODIES), 0.5, 3.0, ((0, 16), (3, 32)), jnp.float32)
    masses = jnp.clip(jnp.exp(math.log(2.0) - 2.3025851 * jax.random.uniform(key_of[2], (BODIES,), jnp.float32) ** shard_levels(key_of[2], (BODIES,), ((0, 32),), -0.2, 0.2)), 0.2, 2.0)
    initial_places = gaussian(key_of[3], (3, BODIES), 1.0, 4.0, ((1, 32),), jnp.float32)
    initial_speeds = gaussian(key_of[4], (3, BODIES), 0.5, 3.0, ((1, 32),), jnp.float32)
    return dict(positions=positions, velocities=velocities, masses=masses, initial_places=initial_places, initial_speeds=initial_speeds)


soften = 0.01
slice_length = 0.25
lobatto_weights = ((5.0 / 24.0, 1.0 / 3.0, -1.0 / 24.0), (-1.0 / 24.0, 1.0 / 3.0, 5.0 / 24.0))

def gravity(places, masses):
    body_count = places.shape[1]
    block = math.gcd(body_count, 512)
    row_blocks = jnp.transpose(places.reshape(3, body_count // block, block), (1, 0, 2))
    weighted = places * masses[None, :]

    def one_block(local_places):
        squared = (places[0][None, :] - local_places[0][:, None]) ** 2
        squared = squared + (places[1][None, :] - local_places[1][:, None]) ** 2
        squared = squared + (places[2][None, :] - local_places[2][:, None]) ** 2
        inverse = lax.rsqrt(squared + soften)
        kernel = inverse * inverse * inverse
        attract = jnp.dot(weighted, kernel.T, precision=lax.Precision.HIGHEST)
        kernel_sum = jnp.dot(masses, kernel.T, precision=lax.Precision.HIGHEST)
        return (attract - local_places * kernel_sum[None, :]) / body_count
    results = lax.map(one_block, row_blocks)
    return jnp.transpose(results, (1, 0, 2)).reshape(3, body_count)

def slice_sweep(places, speeds, masses):
    earlier = [gravity(places[node], masses) for node in range(3)]
    new_places = [places[0]]
    new_speeds = [speeds[0]]
    new_force = [earlier[0]]
    half_step = 0.5 * slice_length
    for node in range(2):
        weights = lobatto_weights[node]
        moved = slice_length * (weights[0] * speeds[0] + weights[1] * speeds[1] + weights[2] * speeds[2])
        kicked = slice_length * (weights[0] * earlier[0] + weights[1] * earlier[1] + weights[2] * earlier[2])
        place = new_places[node] + half_step * (new_speeds[node] - speeds[node]) + moved
        speed = new_speeds[node] + half_step * (new_force[node] - earlier[node]) + kicked
        new_places.append(place)
        new_speeds.append(speed)
        new_force.append(gravity(place, masses))
    drift_place = new_places[2] - (places[0] + slice_length * speeds[0])
    drift_speed = new_speeds[2] - speeds[0]
    return (jnp.stack(new_places[1:]), jnp.stack(new_speeds[1:]), new_force[2], drift_place, drift_speed)

def reference(positions, velocities, masses, initial_places, initial_speeds):

    def per_slice(couple):
        return slice_sweep(couple[0], couple[1], masses)
    node_places, node_speeds, end_force, drift_place, drift_speed = lax.map(per_slice, (positions, velocities))
    carry_place = initial_places
    carry_speed = initial_speeds
    start_list = []
    speed_list = []
    for slice_number in range(SLICES):
        start_list.append(carry_place)
        speed_list.append(carry_speed)
        carry_place = carry_place + slice_length * carry_speed + drift_place[slice_number]
        carry_speed = carry_speed + drift_speed[slice_number]
    return (node_places, node_speeds, end_force, jnp.stack(start_list), jnp.stack(speed_list))
```

```python
import functools

import jax
import jax.numpy as jnp
import numpy as np
from jax import lax
from jax.experimental import pallas as pl
from jax.experimental.pallas import tpu as pltpu
from jax.sharding import PartitionSpec as P

soften = 0.01
slice_length = 0.25
half_step = 0.5 * slice_length
lobatto_weights = ((5.0 / 24.0, 1.0 / 3.0, -1.0 / 24.0), (-1.0 / 24.0, 1.0 / 3.0, 5.0 / 24.0))

bodies = 8192
sources = 32
slices = 16
ring_y, ring_z, cores = 4, 4, 2
f32 = jnp.float32
bf16 = jnp.bfloat16
pull_flops = 2 * 256 * bodies * 256 * 3


def far_groups():
    places = np.arange(sources).reshape(ring_y, ring_z, cores)
    return [[int(p) for p in places[y, :, c]] for y in range(ring_y) for c in range(cores)]


def near_groups():
    places = np.arange(sources).reshape(ring_y, ring_z, cores)
    return [[int(p) for p in places[:, z, :].reshape(-1)] for z in range(ring_z)]


def product(a, b, contract):
    return lax.dot_general(a, b, (contract, ((), ())), preferred_element_type=f32)


def in_three(a):
    high = a.astype(bf16).astype(f32)
    rest = a - high
    middle = rest.astype(bf16).astype(f32)
    low = (rest - middle).astype(bf16).astype(f32)
    return high, middle, low


def own_rows(places):
    squares = jnp.sum(places * places, axis=0, keepdims=True) + soften
    high, middle, low = in_three(-2.0 * places)
    one, zero = jnp.ones_like(squares), jnp.zeros_like(squares)
    return jnp.concatenate(
        [high, high, high, middle, middle, middle, low, low, *in_three(squares), one, one, one, zero, zero], axis=0
    ).astype(bf16)


def far_rows(places):
    squares = jnp.sum(places * places, axis=0, keepdims=True)
    high, middle, low = in_three(places)
    one, zero = jnp.ones_like(squares), jnp.zeros_like(squares)
    return jnp.concatenate(
        [high, middle, low, high, middle, low, high, middle, one, one, one, *in_three(squares), zero, zero], axis=0
    ).astype(bf16)


def weight_rows(places, mass):
    weights = jnp.concatenate([places * mass, mass], axis=0)
    return jnp.concatenate([*in_three(weights), jnp.zeros_like(weights)], axis=0).astype(bf16)


def prepare(node, read, far, weight):
    def one(source, carry):
        places, mass = read(source)
        far[node, source] = far_rows(places)
        weight[node, source] = weight_rows(places, mass)
        return carry

    lax.fori_loop(0, sources, one, 0, unroll=4)


def pulls(owns, far, weight, total, unroll):
    rows = [own_rows(own) for own in owns]
    total[...] = jnp.zeros_like(total)

    def one(source, carry):
        for node in range(len(owns)):
            inverse = lax.rsqrt(product(far[node, source], rows[node], ((0,), (0,))))
            kernel = inverse * inverse * inverse
            high = kernel.astype(bf16)
            low = (kernel - high.astype(f32)).astype(bf16)
            weights = weight[node, source]
            total[node] += product(weights, high, ((1,), (0,))) + product(weights, low, ((1,), (0,)))
        return carry

    lax.fori_loop(0, sources, one, 0, unroll=unroll)
    found = []
    for node, own in enumerate(owns):
        sums = total[node]
        sums = sums[0:4] + sums[4:8] + sums[8:12]
        found.append((sums[0:3] - own * sums[3:4]) * (1.0 / bodies))
    return found


def by_node(array):
    return [jnp.concatenate([array[node, c] for c in range(3)], axis=0) for node in range(3)]


def pack_kernel(positions, velocities, masses, out):
    places, speeds = by_node(positions), by_node(velocities)
    weights = lobatto_weights[0]
    moved = slice_length * (weights[0] * speeds[0] + weights[1] * speeds[1] + weights[2] * speeds[2])
    first = places[0] + moved
    mass = masses[...]
    packed = jnp.concatenate(
        [*places, first, mass, jnp.zeros((3, mass.shape[1]), f32)], axis=0
    )
    for k in range(ring_z):
        out[k] = packed


def old_kernel(packed, own, velocities, out, state, far, weight, total):
    for node in range(3):
        prepare(
            node, lambda s, node=node: (packed[s, 3 * node : 3 * node + 3], packed[s, 12:13]), far, weight
        )
    mine = own[0]
    old = pulls([mine[3 * n : 3 * n + 3] for n in range(3)], far, weight, total, 2)
    speeds = by_node(velocities)
    kicks = [
        slice_length * (w[0] * old[0] + w[1] * old[1] + w[2] * old[2]) for w in lobatto_weights
    ]
    first_speed = speeds[0] + kicks[0]
    weights = lobatto_weights[1]
    moved = slice_length * (weights[0] * speeds[0] + weights[1] * speeds[1] + weights[2] * speeds[2])
    second = mine[9:12] + half_step * (first_speed - speeds[1]) + moved
    for k in range(sources):
        out[k] = second
    state[0] = first_speed
    state[1] = first_speed - half_step * old[1] + kicks[1]
    state[2] = second
    state[3] = second - (mine[0:3] + slice_length * speeds[0])


def middle_kernel(packed, own, velocities, state, places, speeds, drift, far, weight, total):
    prepare(0, lambda s: (packed[s, 9:12], packed[s, 12:13]), far, weight)
    mine = own[0]
    (force,) = pulls([mine[9:12]], far, weight, total, 4)
    last = state[1] + half_step * force
    for c in range(3):
        places[0, c] = jnp.concatenate([mine[9 + c : 10 + c], state[2, c : c + 1]], axis=0)
        speeds[0, c] = jnp.concatenate([state[0, c : c + 1], last[c : c + 1]], axis=0)
    both = jnp.concatenate([state[3], last - by_node(velocities)[0]], axis=0)
    for k in range(slices):
        drift[k] = both


def end_kernel(packed, places, state, out, far, weight, total):
    def read(source):
        other = (source // 8) * 8 + (source % 2) * 4 + (source // 2) % 4
        return places[source], packed[other, 12:13]

    prepare(0, read, far, weight)
    (force,) = pulls([state[2]], far, weight, total, 4)
    for c in range(3):
        out[c] = force[c : c + 1]


def start_kernel(here, drift, places, speeds, start_places, start_speeds):
    me = here[0]
    now = me.astype(f32)
    place = places[...] + (slice_length * now) * speeds[...]
    speed = speeds[...]
    for t in range(slices - 1):
        passed = jnp.where(t < me, 1.0, 0.0)
        kick = drift[t, 3:6] * passed
        place = place + drift[t, 0:3] * passed + (slice_length * (now - (t + 1.0))) * kick
        speed = speed + kick
    for c in range(3):
        start_places[c] = place[c : c + 1]
        start_speeds[c] = speed[c : c + 1]


def run(kernel, outs, scratch=(), smem=0, flops=0):
    cost = pl.CostEstimate(flops=flops, bytes_accessed=0, transcendentals=0) if flops else None

    def call(*args):
        specs = [
            pl.BlockSpec(memory_space=pltpu.SMEM if k < smem else pltpu.VMEM) for k in range(len(args))
        ]
        return pl.pallas_call(
            kernel,
            in_specs=specs,
            out_shape=outs,
            scratch_shapes=list(scratch),
            cost_estimate=cost,
            compiler_params=pltpu.CompilerParams(vmem_limit_bytes=40 * 2**20),
        )(*args)

    return call


def room(nodes):
    return (
        pltpu.VMEM((nodes, sources, 32, 256), bf16),
        pltpu.VMEM((nodes, sources, 16, 256), bf16),
        pltpu.VMEM((nodes, 16, 256), f32),
    )


def copies(array, count):
    return jnp.broadcast_to(array[None], (count, *array.shape))


def shape(*lengths):
    return jax.ShapeDtypeStruct(lengths, f32)


def body(positions, velocities, masses, initial_places, initial_speeds):
    positions = positions.transpose(1, 2, 0, 3)
    velocities = velocities.transpose(1, 2, 0, 3)
    own = run(pack_kernel, shape(ring_z, 16, 256))(positions, velocities, masses[None])
    far = lax.all_to_all(own, "space", 0, 0, axis_index_groups=far_groups(), tiled=True)
    near = copies(far.reshape(ring_z * 16, 256), ring_y * cores)
    near = lax.all_to_all(near, "space", 0, 0, axis_index_groups=near_groups(), tiled=True)
    packed = near.reshape(sources, 16, 256)
    second, state = run(old_kernel, (shape(sources, 3, 256), shape(4, 3, 256)), room(3))(packed, own, velocities)
    gathered = lax.all_to_all(second, "space", 0, 0, tiled=True)
    node_places, node_speeds, drift = run(
        middle_kernel, (shape(1, 3, 2, 256), shape(1, 3, 2, 256), shape(slices, 6, 256)), room(1), flops=pull_flops
    )(packed, own, velocities, state)
    drift, gathered = lax.optimization_barrier((drift, gathered))
    drift = lax.all_to_all(drift, "tm", 0, 0, tiled=True)
    end_force = run(end_kernel, shape(3, 1, 256), room(1), flops=pull_flops)(packed, gathered, state)
    here = lax.axis_index("tm").astype(jnp.int32)[None]
    start_places, start_speeds = run(start_kernel, (shape(3, 1, 256), shape(3, 1, 256)), smem=1)(
        here, drift, initial_places, initial_speeds
    )
    return (
        node_places.transpose(0, 2, 1, 3),
        node_speeds.transpose(0, 2, 1, 3),
        end_force.transpose(1, 0, 2),
        start_places.transpose(1, 0, 2),
        start_speeds.transpose(1, 0, 2),
    )


def solution(mesh):
    return jax.shard_map(
        body,
        mesh=mesh,
        in_specs=(
            P("tm", None, None, "space"),
            P("tm", None, None, "space"),
            P("space"),
            P(None, "space"),
            P(None, "space"),
        ),
        out_specs=(
            P("tm", None, None, "space"),
            P("tm", None, None, "space"),
            P("tm", None, "space"),
            P("tm", None, "space"),
            P("tm", None, "space"),
        ),
        check_vma=False,
    )
```

```python
import jax
import jax.numpy as jnp
import numpy as np
from jax import lax
from jax.experimental import pallas as pl
from jax.experimental.pallas import tpu as pltpu
from jax.sharding import PartitionSpec as P

soften = 0.01
slice_length = 0.25
half_step = 0.5 * slice_length
lobatto_weights = ((5.0 / 24.0, 1.0 / 3.0, -1.0 / 24.0), (-1.0 / 24.0, 1.0 / 3.0, 5.0 / 24.0))

bodies = 8192
sources = 32
slices = 16
ring_y, ring_z, cores = 4, 4, 2
rows_sent = 13
f32 = jnp.float32
bf16 = jnp.bfloat16
pull_flops = 2 * 256 * bodies * 256 * 3


def far_groups():
    places = np.arange(sources).reshape(ring_y, ring_z, cores)
    return [[int(p) for p in places[y, :, c]] for y in range(ring_y) for c in range(cores)]


def near_groups():
    places = np.arange(sources).reshape(ring_y, ring_z, cores)
    return [[int(p) for p in places[:, z, :].reshape(-1)] for z in range(ring_z)]


def product(a, b, contract):
    return lax.dot_general(a, b, (contract, ((), ())), preferred_element_type=f32)


def in_three(a):
    high = a.astype(bf16).astype(f32)
    rest = a - high
    middle = rest.astype(bf16).astype(f32)
    low = (rest - middle).astype(bf16).astype(f32)
    return high, middle, low


def own_rows(places):
    squares = jnp.sum(places * places, axis=0, keepdims=True) + soften
    high, middle, low = in_three(-2.0 * places)
    one, zero = jnp.ones_like(squares), jnp.zeros_like(squares)
    return jnp.concatenate(
        [high, high, high, middle, middle, middle, low, low, *in_three(squares), one, one, one, zero, zero], axis=0
    ).astype(bf16)


def far_rows(places):
    squares = jnp.sum(places * places, axis=0, keepdims=True)
    high, middle, low = in_three(places)
    one, zero = jnp.ones_like(squares), jnp.zeros_like(squares)
    return jnp.concatenate(
        [high, middle, low, high, middle, low, high, middle, one, one, one, *in_three(squares), zero, zero], axis=0
    ).astype(bf16)


def weight_rows(places, mass):
    weights = jnp.concatenate([places * mass, mass], axis=0)
    return jnp.concatenate([*in_three(weights), jnp.zeros_like(weights)], axis=0).astype(bf16)


def pull_from(source, own, weight):
    inverse = lax.rsqrt(product(source, own, ((0,), (0,))))
    kernel = inverse * inverse * inverse
    high = kernel.astype(bf16)
    low = (kernel - high.astype(f32)).astype(bf16)
    return product(weight, high, ((1,), (0,))) + product(weight, low, ((1,), (0,)))


def pulls(owns, read, total, unroll):
    rows = [own_rows(own) for own in owns]
    total[...] = jnp.zeros_like(total)

    def one(near, carry):
        for far in range(ring_z):
            for node in range(len(owns)):
                places, mass = read(node, near, far)
                total[node] += pull_from(far_rows(places), rows[node], weight_rows(places, mass))
        return carry

    lax.fori_loop(0, ring_y * cores, one, 0, unroll=unroll)
    found = []
    for node, own in enumerate(owns):
        sums = total[node]
        sums = sums[0:4] + sums[4:8] + sums[8:12]
        found.append((sums[0:3] - own * sums[3:4]) * (1.0 / bodies))
    return found


def by_node(array):
    return [jnp.concatenate([array[node, c] for c in range(3)], axis=0) for node in range(3)]


def pack_kernel(positions_in, velocities_in, masses_in, out, known, positions, velocities, masses, arrived):
    pairs = ((positions_in, positions), (velocities_in, velocities), (masses_in, masses))
    moves = [pltpu.make_async_copy(a, b, arrived.at[k]) for k, (a, b) in enumerate(pairs)]
    for move in moves:
        move.start()
    for move in moves:
        move.wait()
    places, speeds = by_node(positions), by_node(velocities)
    moved = [slice_length * (w[0] * speeds[0] + w[1] * speeds[1] + w[2] * speeds[2]) for w in lobatto_weights]
    first = places[0] + moved[0]
    packed = jnp.concatenate([*places, first, masses[...]], axis=0)
    for k in range(ring_z):
        out[k] = packed
    known[0] = speeds[0]
    known[1] = first - half_step * speeds[1] + moved[1]
    known[2] = places[0] + slice_length * speeds[0]


def spread_kernel(far, out):
    for k in range(ring_y * cores):
        for z in range(ring_z):
            out[k, rows_sent * z : rows_sent * (z + 1)] = far[z]


def old_kernel(packed, own, known, out, state, total):
    def read(node, near, far):
        at = rows_sent * far
        return packed[near, at + 3 * node : at + 3 * node + 3], packed[near, at + 12 : at + 13]

    mine = own[0]
    old = pulls([mine[3 * n : 3 * n + 3] for n in range(3)], read, total, 4)
    kicks = [slice_length * (w[0] * old[0] + w[1] * old[1] + w[2] * old[2]) for w in lobatto_weights]
    first_speed = known[0] + kicks[0]
    second = known[1] + half_step * first_speed
    halves = [second[:, :128], second[:, 128:]]
    for c in range(3):
        row = jnp.concatenate([half[c : c + 1] for half in halves], axis=0)
        for k in range(sources):
            out[k, c] = row
    state[0] = first_speed
    state[1] = first_speed - half_step * old[1] + kicks[1]
    state[2] = second
    state[3] = second - known[2]


def middle_kernel(packed, own, known, state, places, speeds, drift, total):
    def read(node, near, far):
        at = rows_sent * far
        return packed[near, at + 9 : at + 12], packed[near, at + 12 : at + 13]

    mine = own[0]
    (force,) = pulls([mine[9:12]], read, total, 8)
    last = state[1] + half_step * force
    for c in range(3):
        places[0, c] = jnp.concatenate([mine[9 + c : 10 + c], state[2, c : c + 1]], axis=0)
        speeds[0, c] = jnp.concatenate([state[0, c : c + 1], last[c : c + 1]], axis=0)
    both = jnp.concatenate([state[3], last - known[0]], axis=0)
    for k in range(slices):
        drift[k] = both


def end_kernel(packed, places, state, out, total):
    def read(node, near, far):
        source = (near // cores) * (ring_z * cores) + far * cores + near % cores
        halves = [jnp.concatenate([places[source, c, h : h + 1] for c in range(3)], axis=0) for h in range(2)]
        at = rows_sent * far
        return jnp.concatenate(halves, axis=1), packed[near, at + 12 : at + 13]

    (force,) = pulls([state[2]], read, total, 8)
    for c in range(3):
        out[c] = force[c : c + 1]


def start_kernel(here, drift, places, speeds, start_places, start_speeds):
    me = here[0]
    now = me.astype(f32)
    place = places[...] + (slice_length * now) * speeds[...]
    speed = speeds[...]
    for t in range(slices - 1):
        passed = jnp.where(t < me, 1.0, 0.0)
        kick = drift[t, 3:6] * passed
        place = place + drift[t, 0:3] * passed + (slice_length * (now - (t + 1.0))) * kick
        speed = speed + kick
    for c in range(3):
        start_places[c] = place[c : c + 1]
        start_speeds[c] = speed[c : c + 1]


def run(kernel, outs, places=(), scratch=(), flops=0):
    cost = pl.CostEstimate(flops=flops, bytes_accessed=0, transcendentals=0) if flops else None

    def call(*args):
        specs = [pl.BlockSpec(memory_space=place) for place in places]
        specs += [pl.BlockSpec(memory_space=pltpu.VMEM)] * (len(args) - len(specs))
        return pl.pallas_call(
            kernel,
            in_specs=specs,
            out_shape=outs,
            scratch_shapes=list(scratch),
            cost_estimate=cost,
            compiler_params=pltpu.CompilerParams(vmem_limit_bytes=40 * 2**20),
        )(*args)

    return call


def sums(nodes):
    return (pltpu.VMEM((nodes, 16, 256), f32),)


def shape(*lengths):
    return jax.ShapeDtypeStruct(lengths, f32)


def body(positions, velocities, masses, initial_places, initial_speeds):
    positions = positions.transpose(1, 2, 0, 3)
    velocities = velocities.transpose(1, 2, 0, 3)
    masses = masses[None]
    landing = [pltpu.VMEM(a.shape, f32) for a in (positions, velocities, masses)]
    own, known = run(
        pack_kernel,
        (shape(ring_z, rows_sent, 256), shape(3, 3, 256)),
        places=(pltpu.HBM,) * 3,
        scratch=(*landing, pltpu.SemaphoreType.DMA((3,))),
    )(positions, velocities, masses)
    far = lax.all_to_all(own, "space", 0, 0, axis_index_groups=far_groups(), tiled=True)
    near = run(spread_kernel, shape(ring_y * cores, ring_z * rows_sent, 256))(far)
    packed = lax.all_to_all(near, "space", 0, 0, axis_index_groups=near_groups(), tiled=True)
    second, state = run(old_kernel, (shape(sources, 3, 2, 128), shape(4, 3, 256)), scratch=sums(3))(packed, own, known)
    gathered = lax.all_to_all(second, "space", 0, 0, tiled=True)
    node_places, node_speeds, drift = run(
        middle_kernel,
        (shape(1, 3, 2, 256), shape(1, 3, 2, 256), shape(slices, 6, 256)),
        scratch=sums(1),
        flops=pull_flops,
    )(packed, own, known, state)
    drift, gathered = lax.optimization_barrier((drift, gathered))
    drift = lax.all_to_all(drift, "tm", 0, 0, tiled=True)
    end_force = run(end_kernel, shape(3, 1, 256), scratch=sums(1), flops=pull_flops)(packed, gathered, state)
    here = lax.axis_index("tm").astype(jnp.int32)[None]
    start_places, start_speeds = run(start_kernel, (shape(3, 1, 256), shape(3, 1, 256)), places=(pltpu.SMEM,))(
        here, drift, initial_places, initial_speeds
    )
    return (
        node_places.transpose(0, 2, 1, 3),
        node_speeds.transpose(0, 2, 1, 3),
        end_force.transpose(1, 0, 2),
        start_places.transpose(1, 0, 2),
        start_speeds.transpose(1, 0, 2),
    )


def solution(mesh):
    return jax.shard_map(
        body,
        mesh=mesh,
        in_specs=(
            P("tm", None, None, "space"),
            P("tm", None, None, "space"),
            P("space"),
            P(None, "space"),
            P(None, "space"),
        ),
        out_specs=(
            P("tm", None, None, "space"),
            P("tm", None, None, "space"),
            P("tm", None, "space"),
            P("tm", None, "space"),
            P("tm", None, "space"),
        ),
        check_vma=False,
    )
```

```python
import jax
import jax.numpy as jnp
import numpy as np
from jax import lax
from jax.experimental import pallas as pl
from jax.experimental.pallas import tpu as pltpu
from jax.sharding import PartitionSpec as P

soften = 0.01
slice_length = 0.25
half_step = 0.5 * slice_length
lobatto_weights = ((5.0 / 24.0, 1.0 / 3.0, -1.0 / 24.0), (-1.0 / 24.0, 1.0 / 3.0, 5.0 / 24.0))

bodies = 8192
sources = 32
slices = 16
ring_y, ring_z, cores = 4, 4, 2
line = 4
rows_sent = 13
f32 = jnp.float32
bf16 = jnp.bfloat16
pull_flops = 2 * 256 * bodies * 256 * 3


def far_groups():
    places = np.arange(sources).reshape(ring_y, ring_z, cores)
    return [[int(p) for p in places[y, :, c]] for y in range(ring_y) for c in range(cores)]


def near_groups():
    places = np.arange(sources).reshape(ring_y, ring_z, cores)
    return [[int(p) for p in places[:, z, :].reshape(-1)] for z in range(ring_z)]


def line_groups():
    return [[x * line + k for k in range(line)] for x in range(slices // line)]


def product(a, b, contract):
    return lax.dot_general(a, b, (contract, ((), ())), preferred_element_type=f32)


def in_three(a):
    high = a.astype(bf16).astype(f32)
    rest = a - high
    middle = rest.astype(bf16).astype(f32)
    low = (rest - middle).astype(bf16).astype(f32)
    return high, middle, low


def own_rows(places):
    squares = jnp.sum(places * places, axis=0, keepdims=True) + soften
    high, middle, low = in_three(-2.0 * places)
    one, zero = jnp.ones_like(squares), jnp.zeros_like(squares)
    return jnp.concatenate(
        [high, high, high, middle, middle, middle, low, low, *in_three(squares), one, one, one, zero, zero], axis=0
    ).astype(bf16)


def far_rows(places):
    squares = jnp.sum(places * places, axis=0, keepdims=True)
    high, middle, low = in_three(places)
    one, zero = jnp.ones_like(squares), jnp.zeros_like(squares)
    return jnp.concatenate(
        [high, middle, low, high, middle, low, high, middle, one, one, one, *in_three(squares), zero, zero], axis=0
    ).astype(bf16)


def weight_rows(places, mass):
    weights = jnp.concatenate([places * mass, mass], axis=0)
    return jnp.concatenate([*in_three(weights), jnp.zeros_like(weights)], axis=0).astype(bf16)


def pull_from(source, own, weight):
    inverse = lax.rsqrt(product(source, own, ((0,), (0,))))
    kernel = inverse * inverse * inverse
    high = kernel.astype(bf16)
    low = (kernel - high.astype(f32)).astype(bf16)
    return product(weight, high, ((1,), (0,))) + product(weight, low, ((1,), (0,)))


def pulls(owns, read, total, unroll):
    rows = [own_rows(own) for own in owns]
    total[...] = jnp.zeros_like(total)

    def one(near, carry):
        for far in range(ring_z):
            for node in range(len(owns)):
                places, mass = read(node, near, far)
                total[node] += pull_from(far_rows(places), rows[node], weight_rows(places, mass))
        return carry

    lax.fori_loop(0, ring_y * cores, one, 0, unroll=unroll)
    found = []
    for node, own in enumerate(owns):
        sums = total[node]
        sums = sums[0:4] + sums[4:8] + sums[8:12]
        found.append((sums[0:3] - own * sums[3:4]) * (1.0 / bodies))
    return found


def by_node(array):
    return [jnp.concatenate([array[node, c] for c in range(3)], axis=0) for node in range(3)]


def pack_kernel(positions_in, velocities_in, masses_in, out, known, positions, velocities, masses, arrived):
    pairs = ((positions_in, positions), (velocities_in, velocities), (masses_in, masses))
    moves = [pltpu.make_async_copy(a, b, arrived.at[k]) for k, (a, b) in enumerate(pairs)]
    for move in moves:
        move.start()
    for move in moves:
        move.wait()
    places, speeds = by_node(positions), by_node(velocities)
    moved = [slice_length * (w[0] * speeds[0] + w[1] * speeds[1] + w[2] * speeds[2]) for w in lobatto_weights]
    first = places[0] + moved[0]
    packed = jnp.concatenate([*places, first, masses[...]], axis=0)
    for k in range(ring_z):
        out[k] = packed
    known[0] = speeds[0]
    known[1] = first - half_step * speeds[1] + moved[1]
    known[2] = places[0] + slice_length * speeds[0]


def spread_kernel(far, out):
    for k in range(ring_y * cores):
        for z in range(ring_z):
            out[k, rows_sent * z : rows_sent * (z + 1)] = far[z]


def old_kernel(packed, own, known, out, state, total):
    def read(node, near, far):
        at = rows_sent * far
        return packed[near, at + 3 * node : at + 3 * node + 3], packed[near, at + 12 : at + 13]

    mine = own[0]
    old = pulls([mine[3 * n : 3 * n + 3] for n in range(3)], read, total, 4)
    kicks = [slice_length * (w[0] * old[0] + w[1] * old[1] + w[2] * old[2]) for w in lobatto_weights]
    first_speed = known[0] + kicks[0]
    second = known[1] + half_step * first_speed
    halves = [second[:, :128], second[:, 128:]]
    for c in range(3):
        row = jnp.concatenate([half[c : c + 1] for half in halves], axis=0)
        for k in range(sources):
            out[k, c] = row
    state[0] = first_speed
    state[1] = first_speed - half_step * old[1] + kicks[1]
    state[2] = second
    state[3] = second - known[2]


def middle_kernel(here, packed, own, known, state, places, speeds, drift, total):
    def read(node, near, far):
        at = rows_sent * far
        return packed[near, at + 9 : at + 12], packed[near, at + 12 : at + 13]

    mine = own[0]
    (force,) = pulls([mine[9:12]], read, total, 8)
    last = state[1] + half_step * force
    for c in range(3):
        places[0, c] = jnp.concatenate([mine[9 + c : 10 + c], state[2, c : c + 1]], axis=0)
        speeds[0, c] = jnp.concatenate([state[0, c : c + 1], last[c : c + 1]], axis=0)
    kick = last - known[0]
    drift[0:3] = state[3] - (slice_length * here[0].astype(f32)) * kick
    drift[3:6] = kick


def pair_kernel(here, drift, other, pair, earlier):
    got = other[...]
    pair[...] = drift[...] + got
    earlier[...] = got * jnp.where((here[0] // line) % 2 == 1, 1.0, 0.0)


def four_kernel(here, drift, earlier, other, out):
    passed = earlier[...] + other[...] * jnp.where(here[0] // line >= 2, 1.0, 0.0)
    for k in range(line):
        out[k, 0:6] = passed
        out[k, 6:12] = drift[...]


def end_kernel(packed, places, state, out, total):
    def read(node, near, far):
        source = (near // cores) * (ring_z * cores) + far * cores + near % cores
        halves = [jnp.concatenate([places[source, c, h : h + 1] for c in range(3)], axis=0) for h in range(2)]
        at = rows_sent * far
        return jnp.concatenate(halves, axis=1), packed[near, at + 12 : at + 13]

    (force,) = pulls([state[2]], read, total, 8)
    for c in range(3):
        out[c] = force[c : c + 1]


def start_kernel(here, drift, places, speeds, start_places, start_speeds):
    now = here[0].astype(f32)
    mine = here[0] % line
    passed = jnp.zeros((6, drift.shape[2]), f32)
    for k in range(line):
        passed = passed + drift[k, 0:6] + drift[k, 6:12] * jnp.where(k < mine, 1.0, 0.0)
    kick = passed[3:6]
    place = places[...] + (slice_length * now) * speeds[...] + passed[0:3] + (slice_length * (now - 1.0)) * kick
    speed = speeds[...] + kick
    for c in range(3):
        start_places[c] = place[c : c + 1]
        start_speeds[c] = speed[c : c + 1]


def run(kernel, outs, places=(), scratch=(), flops=0, room=40):
    cost = pl.CostEstimate(flops=flops, bytes_accessed=0, transcendentals=0) if flops else None

    def call(*args):
        specs = [pl.BlockSpec(memory_space=place) for place in places]
        specs += [pl.BlockSpec(memory_space=pltpu.VMEM)] * (len(args) - len(specs))
        return pl.pallas_call(
            kernel,
            in_specs=specs,
            out_shape=outs,
            scratch_shapes=list(scratch),
            cost_estimate=cost,
            compiler_params=pltpu.CompilerParams(vmem_limit_bytes=room * 2**20),
        )(*args)

    return call


def sums(nodes):
    return (pltpu.VMEM((nodes, 16, 256), f32),)


def shape(*lengths):
    return jax.ShapeDtypeStruct(lengths, f32)


def body(positions, velocities, masses, initial_places, initial_speeds):
    positions = positions.transpose(1, 2, 0, 3)
    velocities = velocities.transpose(1, 2, 0, 3)
    masses = masses[None]
    landing = [pltpu.VMEM(a.shape, f32) for a in (positions, velocities, masses)]
    own, known = run(
        pack_kernel,
        (shape(ring_z, rows_sent, 256), shape(3, 3, 256)),
        places=(pltpu.HBM,) * 3,
        scratch=(*landing, pltpu.SemaphoreType.DMA((3,))),
        room=60,
    )(positions, velocities, masses)
    far = lax.all_to_all(own, "space", 0, 0, axis_index_groups=far_groups(), tiled=True)
    near = run(spread_kernel, shape(ring_y * cores, ring_z * rows_sent, 256))(far)
    packed = lax.all_to_all(near, "space", 0, 0, axis_index_groups=near_groups(), tiled=True)
    second, state = run(old_kernel, (shape(sources, 3, 2, 128), shape(4, 3, 256)), scratch=sums(3))(packed, own, known)
    gathered = lax.all_to_all(second, "space", 0, 0, tiled=True)
    here = lax.axis_index("tm").astype(jnp.int32)[None]
    node_places, node_speeds, drift = run(
        middle_kernel,
        (shape(1, 3, 2, 256), shape(1, 3, 2, 256), shape(6, 256)),
        places=(pltpu.SMEM,),
        scratch=sums(1),
        flops=pull_flops,
    )(here, packed, own, known, state)
    other = lax.ppermute(drift, "tm", [(t, t ^ line) for t in range(slices)])
    pair, earlier = run(pair_kernel, (shape(6, 256), shape(6, 256)), places=(pltpu.SMEM,))(here, drift, other)
    other = lax.ppermute(pair, "tm", [(t, t ^ (2 * line)) for t in range(slices)])
    drift = run(four_kernel, shape(line, 12, 256), places=(pltpu.SMEM,))(here, drift, earlier, other)
    drift, gathered = lax.optimization_barrier((drift, gathered))
    drift = lax.all_to_all(drift, "tm", 0, 0, axis_index_groups=line_groups(), tiled=True)
    end_force = run(end_kernel, shape(3, 1, 256), scratch=sums(1), flops=pull_flops)(packed, gathered, state)
    start_places, start_speeds = run(start_kernel, (shape(3, 1, 256), shape(3, 1, 256)), places=(pltpu.SMEM,))(
        here, drift, initial_places, initial_speeds
    )
    return (
        node_places.transpose(0, 2, 1, 3),
        node_speeds.transpose(0, 2, 1, 3),
        end_force.transpose(1, 0, 2),
        start_places.transpose(1, 0, 2),
        start_speeds.transpose(1, 0, 2),
    )


def solution(mesh):
    return jax.shard_map(
        body,
        mesh=mesh,
        in_specs=(
            P("tm", None, None, "space"),
            P("tm", None, None, "space"),
            P("space"),
            P(None, "space"),
            P(None, "space"),
        ),
        out_specs=(
            P("tm", None, None, "space"),
            P("tm", None, None, "space"),
            P("tm", None, "space"),
            P("tm", None, "space"),
            P("tm", None, "space"),
        ),
        check_vma=False,
    )
```

```python
import jax
import jax.numpy as jnp
import numpy as np
from jax import lax
from jax.experimental import pallas as pl
from jax.experimental.pallas import tpu as pltpu
from jax.sharding import PartitionSpec as P

soften = 0.01
slice_length = 0.25
half_step = 0.5 * slice_length
lobatto_weights = ((5.0 / 24.0, 1.0 / 3.0, -1.0 / 24.0), (-1.0 / 24.0, 1.0 / 3.0, 5.0 / 24.0))

bodies = 8192
sources = 32
slices = 16
ring_y, ring_z, cores = 4, 4, 2
line = 4
rows_sent = 13
f32 = jnp.float32
bf16 = jnp.bfloat16
pull_flops = 2 * 256 * bodies * 256 * 3


def far_groups():
    places = np.arange(sources).reshape(ring_y, ring_z, cores)
    return [[int(p) for p in places[y, :, c]] for y in range(ring_y) for c in range(cores)]


def near_groups():
    places = np.arange(sources).reshape(ring_y, ring_z, cores)
    return [[int(p) for p in places[:, z, :].reshape(-1)] for z in range(ring_z)]


def line_groups():
    return [[x * line + k for k in range(line)] for x in range(slices // line)]


def product(a, b, contract):
    return lax.dot_general(a, b, (contract, ((), ())), preferred_element_type=f32)


def in_three(a):
    high = a.astype(bf16).astype(f32)
    rest = a - high
    middle = rest.astype(bf16).astype(f32)
    low = (rest - middle).astype(bf16).astype(f32)
    return high, middle, low


def own_rows(places):
    squares = jnp.sum(places * places, axis=0, keepdims=True) + soften
    high, middle, low = in_three(-2.0 * places)
    one, zero = jnp.ones_like(squares), jnp.zeros_like(squares)
    return jnp.concatenate(
        [high, high, high, middle, middle, middle, low, low, *in_three(squares), one, one, one, zero, zero], axis=0
    ).astype(bf16)


def far_rows(places):
    squares = jnp.sum(places * places, axis=0, keepdims=True)
    high, middle, low = in_three(places)
    one, zero = jnp.ones_like(squares), jnp.zeros_like(squares)
    return jnp.concatenate(
        [high, middle, low, high, middle, low, high, middle, one, one, one, *in_three(squares), zero, zero], axis=0
    ).astype(bf16)


def weight_rows(places, mass):
    weights = jnp.concatenate([places * mass, mass], axis=0)
    return jnp.concatenate([*in_three(weights), jnp.zeros_like(weights)], axis=0).astype(bf16)


def pull_from(source, own, weight):
    inverse = lax.rsqrt(product(source, own, ((0,), (0,))))
    kernel = inverse * inverse * inverse
    high = kernel.astype(bf16)
    low = (kernel - high.astype(f32)).astype(bf16)
    return product(weight, high, ((1,), (0,))) + product(weight, low, ((1,), (0,)))


def add_pulls(owns, read, blocks, total):
    rows = [own_rows(own) for own in owns]

    def one(block, carry):
        for far in range(ring_z):
            for node in range(len(owns)):
                places, mass = read(node, block, far)
                total[node] += pull_from(far_rows(places), rows[node], weight_rows(places, mass))
        return carry

    lax.fori_loop(0, blocks, one, 0, unroll=blocks)


def forces(owns, total):
    found = []
    for node, own in enumerate(owns):
        sums = total[node]
        sums = sums[0:4] + sums[4:8] + sums[8:12]
        found.append((sums[0:3] - own * sums[3:4]) * (1.0 / bodies))
    return found


def pulls(owns, read, total):
    total[...] = jnp.zeros_like(total)
    add_pulls(owns, read, ring_y * cores, total)
    return forces(owns, total)


def by_node(array):
    return [jnp.concatenate([array[node, c] for c in range(3)], axis=0) for node in range(3)]


def pack_kernel(positions_in, velocities_in, masses_in, out, known, positions, velocities, masses, arrived):
    pairs = ((positions_in, positions), (velocities_in, velocities), (masses_in, masses))
    moves = [pltpu.make_async_copy(a, b, arrived.at[k]) for k, (a, b) in enumerate(pairs)]
    for move in moves:
        move.start()
    for move in moves:
        move.wait()
    places, speeds = by_node(positions), by_node(velocities)
    moved = [slice_length * (w[0] * speeds[0] + w[1] * speeds[1] + w[2] * speeds[2]) for w in lobatto_weights]
    first = places[0] + moved[0]
    packed = jnp.concatenate([*places, first, masses[...]], axis=0)
    for k in range(ring_z):
        out[k] = packed
    known[0] = speeds[0]
    known[1] = first - half_step * speeds[1] + moved[1]
    known[2] = places[0] + slice_length * speeds[0]


def spread_kernel(far, out):
    for k in range(ring_y * cores):
        for z in range(ring_z):
            out[k, rows_sent * z : rows_sent * (z + 1)] = far[z]


def nodes_of(mine):
    return [mine[3 * n : 3 * n + 3] for n in range(3)]


def column_kernel(far, own, total):
    def read(node, block, z):
        return far[z, 3 * node : 3 * node + 3], far[z, 12:13]

    total[...] = jnp.zeros_like(total)
    add_pulls(nodes_of(own[0]), read, 1, total)


def old_kernel(here, packed, own, known, column, out, state, total):
    def read(node, block, far):
        near = (here[0] + block + 1) % (ring_y * cores)
        at = rows_sent * far
        return packed[near, at + 3 * node : at + 3 * node + 3], packed[near, at + 12 : at + 13]

    total[...] = column[...]
    owns = nodes_of(own[0])
    add_pulls(owns, read, ring_y * cores - 1, total)
    old = forces(owns, total)
    kicks = [slice_length * (w[0] * old[0] + w[1] * old[1] + w[2] * old[2]) for w in lobatto_weights]
    first_speed = known[0] + kicks[0]
    second = known[1] + half_step * first_speed
    halves = [second[:, :128], second[:, 128:]]
    for c in range(3):
        row = jnp.concatenate([half[c : c + 1] for half in halves], axis=0)
        for k in range(sources):
            out[k, c] = row
    state[0] = first_speed
    state[1] = first_speed - half_step * old[1] + kicks[1]
    state[2] = second
    state[3] = second - known[2]


def middle_kernel(here, packed, own, known, state, places, speeds, drift, total):
    def read(node, near, far):
        at = rows_sent * far
        return packed[near, at + 9 : at + 12], packed[near, at + 12 : at + 13]

    mine = own[0]
    (force,) = pulls([mine[9:12]], read, total)
    last = state[1] + half_step * force
    for c in range(3):
        places[0, c] = jnp.concatenate([mine[9 + c : 10 + c], state[2, c : c + 1]], axis=0)
        speeds[0, c] = jnp.concatenate([state[0, c : c + 1], last[c : c + 1]], axis=0)
    kick = last - known[0]
    drift[0:3] = state[3] - (slice_length * here[0].astype(f32)) * kick
    drift[3:6] = kick


def pair_kernel(here, drift, other, pair, earlier):
    got = other[...]
    pair[...] = drift[...] + got
    earlier[...] = got * jnp.where((here[0] // line) % 2 == 1, 1.0, 0.0)


def four_kernel(here, drift, earlier, other, out):
    passed = earlier[...] + other[...] * jnp.where(here[0] // line >= 2, 1.0, 0.0)
    for k in range(line):
        out[k, 0:6] = passed
        out[k, 6:12] = drift[...]


def end_kernel(packed, places, state, out, total):
    def read(node, near, far):
        source = (near // cores) * (ring_z * cores) + far * cores + near % cores
        halves = [jnp.concatenate([places[source, c, h : h + 1] for c in range(3)], axis=0) for h in range(2)]
        at = rows_sent * far
        return jnp.concatenate(halves, axis=1), packed[near, at + 12 : at + 13]

    (force,) = pulls([state[2]], read, total)
    for c in range(3):
        out[c] = force[c : c + 1]


def start_kernel(here, drift, places, speeds, start_places, start_speeds):
    now = here[0].astype(f32)
    mine = here[0] % line
    passed = jnp.zeros((6, drift.shape[2]), f32)
    for k in range(line):
        passed = passed + drift[k, 0:6] + drift[k, 6:12] * jnp.where(k < mine, 1.0, 0.0)
    kick = passed[3:6]
    place = places[...] + (slice_length * now) * speeds[...] + passed[0:3] + (slice_length * (now - 1.0)) * kick
    speed = speeds[...] + kick
    for c in range(3):
        start_places[c] = place[c : c + 1]
        start_speeds[c] = speed[c : c + 1]


def run(kernel, outs, places=(), scratch=(), flops=0, room=40):
    cost = pl.CostEstimate(flops=flops, bytes_accessed=0, transcendentals=0) if flops else None

    def call(*args):
        specs = [pl.BlockSpec(memory_space=place) for place in places]
        specs += [pl.BlockSpec(memory_space=pltpu.VMEM)] * (len(args) - len(specs))
        return pl.pallas_call(
            kernel,
            in_specs=specs,
            out_shape=outs,
            scratch_shapes=list(scratch),
            cost_estimate=cost,
            compiler_params=pltpu.CompilerParams(vmem_limit_bytes=room * 2**20),
        )(*args)

    return call


def sums(nodes):
    return (pltpu.VMEM((nodes, 16, 256), f32),)


def shape(*lengths):
    return jax.ShapeDtypeStruct(lengths, f32)


def body(positions, velocities, masses, initial_places, initial_speeds):
    positions = positions.transpose(1, 2, 0, 3)
    velocities = velocities.transpose(1, 2, 0, 3)
    masses = masses[None]
    landing = [pltpu.VMEM(a.shape, f32) for a in (positions, velocities, masses)]
    own, known = run(
        pack_kernel,
        (shape(ring_z, rows_sent, 256), shape(3, 3, 256)),
        places=(pltpu.HBM,) * 3,
        scratch=(*landing, pltpu.SemaphoreType.DMA((3,))),
        room=60,
    )(positions, velocities, masses)
    far = lax.all_to_all(own, "space", 0, 0, axis_index_groups=far_groups(), tiled=True)
    near = run(spread_kernel, shape(ring_y * cores, ring_z * rows_sent, 256))(far)
    packed = lax.all_to_all(near, "space", 0, 0, axis_index_groups=near_groups(), tiled=True)
    column = run(column_kernel, shape(3, 16, 256), flops=pull_flops)(far, own)
    place = lax.axis_index("space").astype(jnp.int32)
    place = ((place // (ring_z * cores)) * cores + place % cores)[None]
    second, state = run(
        old_kernel, (shape(sources, 3, 2, 128), shape(4, 3, 256)), places=(pltpu.SMEM,), scratch=sums(3)
    )(place, packed, own, known, column)
    gathered = lax.all_to_all(second, "space", 0, 0, tiled=True)
    here = lax.axis_index("tm").astype(jnp.int32)[None]
    node_places, node_speeds, drift = run(
        middle_kernel,
        (shape(1, 3, 2, 256), shape(1, 3, 2, 256), shape(6, 256)),
        places=(pltpu.SMEM,),
        scratch=sums(1),
        flops=pull_flops,
    )(here, packed, own, known, state)
    other = lax.ppermute(drift, "tm", [(t, t ^ line) for t in range(slices)])
    pair, earlier = run(pair_kernel, (shape(6, 256), shape(6, 256)), places=(pltpu.SMEM,))(here, drift, other)
    other = lax.ppermute(pair, "tm", [(t, t ^ (2 * line)) for t in range(slices)])
    drift = run(four_kernel, shape(line, 12, 256), places=(pltpu.SMEM,))(here, drift, earlier, other)
    drift, gathered = lax.optimization_barrier((drift, gathered))
    drift = lax.all_to_all(drift, "tm", 0, 0, axis_index_groups=line_groups(), tiled=True)
    end_force = run(end_kernel, shape(3, 1, 256), scratch=sums(1), flops=pull_flops)(packed, gathered, state)
    start_places, start_speeds = run(start_kernel, (shape(3, 1, 256), shape(3, 1, 256)), places=(pltpu.SMEM,))(
        here, drift, initial_places, initial_speeds
    )
    return (
        node_places.transpose(0, 2, 1, 3),
        node_speeds.transpose(0, 2, 1, 3),
        end_force.transpose(1, 0, 2),
        start_places.transpose(1, 0, 2),
        start_speeds.transpose(1, 0, 2),
    )


def solution(mesh):
    return jax.shard_map(
        body,
        mesh=mesh,
        in_specs=(
            P("tm", None, None, "space"),
            P("tm", None, None, "space"),
            P("space"),
            P(None, "space"),
            P(None, "space"),
        ),
        out_specs=(
            P("tm", None, None, "space"),
            P("tm", None, None, "space"),
            P("tm", None, "space"),
            P("tm", None, "space"),
            P("tm", None, "space"),
        ),
        check_vma=False,
    )
```

```python
import jax
import jax.numpy as jnp
import numpy as np
from jax import lax
from jax.experimental import pallas as pl
from jax.experimental.pallas import tpu as pltpu
from jax.sharding import PartitionSpec as P

soften = 0.01
slice_length = 0.25
half_step = 0.5 * slice_length
lobatto_weights = ((5.0 / 24.0, 1.0 / 3.0, -1.0 / 24.0), (-1.0 / 24.0, 1.0 / 3.0, 5.0 / 24.0))

bodies = 8192
sources = 32
slices = 16
ring_y, ring_z, cores = 4, 4, 2
line = 4
rows_sent = 13
f32 = jnp.float32
bf16 = jnp.bfloat16
pull_flops = 2 * 256 * bodies * 256 * 3


def far_groups():
    places = np.arange(sources).reshape(ring_y, ring_z, cores)
    return [[int(p) for p in places[y, :, c]] for y in range(ring_y) for c in range(cores)]


def near_groups():
    places = np.arange(sources).reshape(ring_y, ring_z, cores)
    return [[int(p) for p in places[:, z, :].reshape(-1)] for z in range(ring_z)]


def line_groups():
    return [[x * line + k for k in range(line)] for x in range(slices // line)]


def product(a, b, contract):
    return lax.dot_general(a, b, (contract, ((), ())), preferred_element_type=f32)


def in_three(a):
    high = a.astype(bf16).astype(f32)
    rest = a - high
    middle = rest.astype(bf16).astype(f32)
    low = (rest - middle).astype(bf16).astype(f32)
    return high, middle, low


def own_rows(places):
    squares = jnp.sum(places * places, axis=0, keepdims=True) + soften
    high, middle, low = in_three(-2.0 * places)
    one, zero = jnp.ones_like(squares), jnp.zeros_like(squares)
    return jnp.concatenate(
        [high, high, high, middle, middle, middle, low, low, *in_three(squares), one, one, one, zero, zero], axis=0
    ).astype(bf16)


def far_rows(places):
    squares = jnp.sum(places * places, axis=0, keepdims=True)
    high, middle, low = in_three(places)
    one, zero = jnp.ones_like(squares), jnp.zeros_like(squares)
    return jnp.concatenate(
        [high, middle, low, high, middle, low, high, middle, one, one, one, *in_three(squares), zero, zero], axis=0
    ).astype(bf16)


def weight_rows(places, mass):
    weights = jnp.concatenate([places * mass, mass], axis=0)
    return jnp.concatenate([*in_three(weights), jnp.zeros_like(weights)], axis=0).astype(bf16)


def pull_from(source, own, weight):
    inverse = lax.rsqrt(product(source, own, ((0,), (0,))))
    kernel = inverse * inverse * inverse
    high = kernel.astype(bf16)
    low = (kernel - high.astype(f32)).astype(bf16)
    return product(weight, high, ((1,), (0,))) + product(weight, low, ((1,), (0,)))


def add_pulls(owns, read, blocks, total):
    rows = [own_rows(own) for own in owns]

    def one(block, carry):
        for far in range(ring_z):
            for node in range(len(owns)):
                places, mass = read(node, block, far)
                total[node] += pull_from(far_rows(places), rows[node], weight_rows(places, mass))
        return carry

    lax.fori_loop(0, blocks, one, 0, unroll=blocks)


def forces(owns, total):
    found = []
    for node, own in enumerate(owns):
        sums = total[node]
        sums = sums[0:4] + sums[4:8] + sums[8:12]
        found.append((sums[0:3] - own * sums[3:4]) * (1.0 / bodies))
    return found


def pulls(owns, read, total):
    total[...] = jnp.zeros_like(total)
    add_pulls(owns, read, ring_y * cores, total)
    return forces(owns, total)


def by_node(array):
    return [jnp.concatenate([array[node, c] for c in range(3)], axis=0) for node in range(3)]


def pack_kernel(positions_in, velocities_in, masses_in, out, known, positions, velocities, masses, arrived):
    pairs = ((positions_in, positions), (velocities_in, velocities), (masses_in, masses))
    moves = [pltpu.make_async_copy(a, b, arrived.at[k]) for k, (a, b) in enumerate(pairs)]
    for move in moves:
        move.start()
    for move in moves:
        move.wait()
    places, speeds = by_node(positions), by_node(velocities)
    moved = [slice_length * (w[0] * speeds[0] + w[1] * speeds[1] + w[2] * speeds[2]) for w in lobatto_weights]
    first = places[0] + moved[0]
    packed = jnp.concatenate([*places, first, masses[...]], axis=0)
    for k in range(ring_z):
        out[k] = packed
    known[0] = speeds[0]
    known[1] = first - half_step * speeds[1] + moved[1]
    known[2] = places[0] + slice_length * speeds[0]


def spread_kernel(far, out):
    for k in range(ring_y * cores):
        for z in range(ring_z):
            out[k, rows_sent * z : rows_sent * (z + 1)] = far[z]


def nodes_of(mine, count):
    return [mine[3 * n : 3 * n + 3] for n in range(count)]


def near_block(here, block):
    return (here[0] + block + 1) % (ring_y * cores)


def column_kernel(far, own, total):
    def read(node, block, z):
        return far[z, 3 * node : 3 * node + 3], far[z, 12:13]

    total[...] = jnp.zeros_like(total)
    add_pulls(nodes_of(own[0], 4), read, 1, total)


def old_kernel(here, packed, own, known, column, out, state, total):
    def read(node, block, far):
        near = near_block(here, block)
        at = rows_sent * far
        return packed[near, at + 3 * node : at + 3 * node + 3], packed[near, at + 12 : at + 13]

    total[...] = column[0:3]
    owns = nodes_of(own[0], 3)
    add_pulls(owns, read, ring_y * cores - 1, total)
    old = forces(owns, total)
    kicks = [slice_length * (w[0] * old[0] + w[1] * old[1] + w[2] * old[2]) for w in lobatto_weights]
    first_speed = known[0] + kicks[0]
    second = known[1] + half_step * first_speed
    halves = [second[:, :128], second[:, 128:]]
    for c in range(3):
        row = jnp.concatenate([half[c : c + 1] for half in halves], axis=0)
        for k in range(sources):
            out[k, c] = row
    state[0] = first_speed
    state[1] = first_speed - half_step * old[1] + kicks[1]
    state[2] = second
    state[3] = second - known[2]


def middle_kernel(here, now, packed, own, known, state, column, places, speeds, drift, total):
    def read(node, block, far):
        near = near_block(here, block)
        at = rows_sent * far
        return packed[near, at + 9 : at + 12], packed[near, at + 12 : at + 13]

    mine = own[0]
    total[...] = column[3:4]
    owns = [mine[9:12]]
    add_pulls(owns, read, ring_y * cores - 1, total)
    (force,) = forces(owns, total)
    last = state[1] + half_step * force
    for c in range(3):
        places[0, c] = jnp.concatenate([mine[9 + c : 10 + c], state[2, c : c + 1]], axis=0)
        speeds[0, c] = jnp.concatenate([state[0, c : c + 1], last[c : c + 1]], axis=0)
    kick = last - known[0]
    drift[0:3] = state[3] - (slice_length * now[0].astype(f32)) * kick
    drift[3:6] = kick


def line_kernel(now, drift, *others_and_out):
    *others, out = others_and_out
    x = now[0] // line
    mine = drift[...]
    passed = jnp.zeros_like(mine)
    for k, other in enumerate(others):
        passed = passed + other[...] * jnp.where((x ^ (k + 1)) < x, 1.0, 0.0)
    for k in range(line):
        out[k, 0:6] = passed
        out[k, 6:12] = mine


def end_kernel(packed, places, state, out, total):
    def read(node, near, far):
        source = (near // cores) * (ring_z * cores) + far * cores + near % cores
        halves = [jnp.concatenate([places[source, c, h : h + 1] for c in range(3)], axis=0) for h in range(2)]
        at = rows_sent * far
        return jnp.concatenate(halves, axis=1), packed[near, at + 12 : at + 13]

    (force,) = pulls([state[2]], read, total)
    for c in range(3):
        out[c] = force[c : c + 1]


def start_kernel(here, drift, places, speeds, start_places, start_speeds):
    now = here[0].astype(f32)
    mine = here[0] % line
    passed = jnp.zeros((6, drift.shape[2]), f32)
    for k in range(line):
        passed = passed + drift[k, 0:6] + drift[k, 6:12] * jnp.where(k < mine, 1.0, 0.0)
    kick = passed[3:6]
    place = places[...] + (slice_length * now) * speeds[...] + passed[0:3] + (slice_length * (now - 1.0)) * kick
    speed = speeds[...] + kick
    for c in range(3):
        start_places[c] = place[c : c + 1]
        start_speeds[c] = speed[c : c + 1]


def run(kernel, outs, places=(), scratch=(), flops=0, room=40):
    cost = pl.CostEstimate(flops=flops, bytes_accessed=0, transcendentals=0) if flops else None

    def call(*args):
        specs = [pl.BlockSpec(memory_space=place) for place in places]
        specs += [pl.BlockSpec(memory_space=pltpu.VMEM)] * (len(args) - len(specs))
        return pl.pallas_call(
            kernel,
            in_specs=specs,
            out_shape=outs,
            scratch_shapes=list(scratch),
            cost_estimate=cost,
            compiler_params=pltpu.CompilerParams(vmem_limit_bytes=room * 2**20),
        )(*args)

    return call


def sums(nodes):
    return (pltpu.VMEM((nodes, 16, 256), f32),)


def shape(*lengths):
    return jax.ShapeDtypeStruct(lengths, f32)


def body(positions, velocities, masses, initial_places, initial_speeds):
    positions = positions.transpose(1, 2, 0, 3)
    velocities = velocities.transpose(1, 2, 0, 3)
    masses = masses[None]
    landing = [pltpu.VMEM(a.shape, f32) for a in (positions, velocities, masses)]
    own, known = run(
        pack_kernel,
        (shape(ring_z, rows_sent, 256), shape(3, 3, 256)),
        places=(pltpu.HBM,) * 3,
        scratch=(*landing, pltpu.SemaphoreType.DMA((3,))),
        room=60,
    )(positions, velocities, masses)
    far = lax.all_to_all(own, "space", 0, 0, axis_index_groups=far_groups(), tiled=True)
    near = run(spread_kernel, shape(ring_y * cores, ring_z * rows_sent, 256))(far)
    packed = lax.all_to_all(near, "space", 0, 0, axis_index_groups=near_groups(), tiled=True)
    column = run(column_kernel, shape(4, 16, 256), flops=pull_flops)(far, own)
    place = lax.axis_index("space").astype(jnp.int32)
    place = ((place // (ring_z * cores)) * cores + place % cores)[None]
    second, state = run(
        old_kernel, (shape(sources, 3, 2, 128), shape(4, 3, 256)), places=(pltpu.SMEM,), scratch=sums(3)
    )(place, packed, own, known, column)
    gathered = lax.all_to_all(second, "space", 0, 0, tiled=True)
    now = lax.axis_index("tm").astype(jnp.int32)[None]
    node_places, node_speeds, drift = run(
        middle_kernel,
        (shape(1, 3, 2, 256), shape(1, 3, 2, 256), shape(6, 256)),
        places=(pltpu.SMEM, pltpu.SMEM),
        scratch=sums(1),
        flops=pull_flops,
    )(place, now, packed, own, known, state, column)
    others = [
        lax.ppermute(drift, "tm", [(t, t ^ (k * line)) for t in range(slices)]) for k in range(1, slices // line)
    ]
    drift = run(line_kernel, shape(line, 12, 256), places=(pltpu.SMEM,))(now, drift, *others)
    drift, gathered = lax.optimization_barrier((drift, gathered))
    drift = lax.all_to_all(drift, "tm", 0, 0, axis_index_groups=line_groups(), tiled=True)
    end_force = run(end_kernel, shape(3, 1, 256), scratch=sums(1), flops=pull_flops)(packed, gathered, state)
    start_places, start_speeds = run(start_kernel, (shape(3, 1, 256), shape(3, 1, 256)), places=(pltpu.SMEM,))(
        now, drift, initial_places, initial_speeds
    )
    return (
        node_places.transpose(0, 2, 1, 3),
        node_speeds.transpose(0, 2, 1, 3),
        end_force.transpose(1, 0, 2),
        start_places.transpose(1, 0, 2),
        start_speeds.transpose(1, 0, 2),
    )


def solution(mesh):
    return jax.shard_map(
        body,
        mesh=mesh,
        in_specs=(
            P("tm", None, None, "space"),
            P("tm", None, None, "space"),
            P("space"),
            P(None, "space"),
            P(None, "space"),
        ),
        out_specs=(
            P("tm", None, None, "space"),
            P("tm", None, None, "space"),
            P("tm", None, "space"),
            P("tm", None, "space"),
            P("tm", None, "space"),
        ),
        check_vma=False,
    )
```

```python
import jax
import jax.numpy as jnp
import numpy as np
from jax import lax
from jax.experimental import pallas as pl
from jax.experimental.pallas import tpu as pltpu
from jax.sharding import PartitionSpec as P

soften = 0.01
slice_length = 0.25
half_step = 0.5 * slice_length
lobatto_weights = ((5.0 / 24.0, 1.0 / 3.0, -1.0 / 24.0), (-1.0 / 24.0, 1.0 / 3.0, 5.0 / 24.0))

bodies = 8192
sources = 32
slices = 16
ring_y, ring_z, cores = 4, 4, 2
line = 4
rows_sent = 13
f32 = jnp.float32
bf16 = jnp.bfloat16
pull_flops = 2 * 256 * bodies * 256 * 3


def far_groups():
    places = np.arange(sources).reshape(ring_y, ring_z, cores)
    return [[int(p) for p in places[y, :, c]] for y in range(ring_y) for c in range(cores)]


def near_groups():
    places = np.arange(sources).reshape(ring_y, ring_z, cores)
    return [[int(p) for p in places[:, z, :].reshape(-1)] for z in range(ring_z)]


def line_groups():
    return [[x * line + k for k in range(line)] for x in range(slices // line)]


def product(a, b, contract):
    return lax.dot_general(a, b, (contract, ((), ())), preferred_element_type=f32)


def in_three(a):
    high = a.astype(bf16).astype(f32)
    rest = a - high
    middle = rest.astype(bf16).astype(f32)
    low = (rest - middle).astype(bf16).astype(f32)
    return high, middle, low


def own_rows(places):
    squares = jnp.sum(places * places, axis=0, keepdims=True) + soften
    high, middle, low = in_three(-2.0 * places)
    one, zero = jnp.ones_like(squares), jnp.zeros_like(squares)
    return jnp.concatenate(
        [high, high, high, middle, middle, middle, low, low, *in_three(squares), one, one, one, zero, zero], axis=0
    ).astype(bf16)


def far_rows(places):
    squares = jnp.sum(places * places, axis=0, keepdims=True)
    high, middle, low = in_three(places)
    one, zero = jnp.ones_like(squares), jnp.zeros_like(squares)
    return jnp.concatenate(
        [high, middle, low, high, middle, low, high, middle, one, one, one, *in_three(squares), zero, zero], axis=0
    ).astype(bf16)


def weight_rows(places, mass):
    weights = jnp.concatenate([places * mass, mass], axis=0)
    return jnp.concatenate([*in_three(weights), jnp.zeros_like(weights)], axis=0).astype(bf16)


def pull_from(source, own, weight):
    inverse = lax.rsqrt(product(source, own, ((0,), (0,))))
    kernel = inverse * inverse * inverse
    high = kernel.astype(bf16)
    low = (kernel - high.astype(f32)).astype(bf16)
    return product(weight, high, ((1,), (0,))) + product(weight, low, ((1,), (0,)))


def add_pulls(owns, read, blocks, total):
    rows = [own_rows(own) for own in owns]

    def one(block, carry):
        for far in range(ring_z):
            for node in range(len(owns)):
                places, mass = read(node, block, far)
                total[node] += pull_from(far_rows(places), rows[node], weight_rows(places, mass))
        return carry

    lax.fori_loop(0, blocks, one, 0, unroll=blocks)


def forces(owns, total):
    found = []
    for node, own in enumerate(owns):
        sums = total[node]
        sums = sums[0:4] + sums[4:8] + sums[8:12]
        found.append((sums[0:3] - own * sums[3:4]) * (1.0 / bodies))
    return found


def pulls(owns, read, total):
    total[...] = jnp.zeros_like(total)
    add_pulls(owns, read, ring_y * cores, total)
    return forces(owns, total)


def by_node(array):
    return [jnp.concatenate([array[node, c] for c in range(3)], axis=0) for node in range(3)]


def pack_kernel(positions_in, velocities_in, masses_in, out, known, positions, velocities, masses, arrived):
    pairs = ((positions_in, positions), (velocities_in, velocities), (masses_in, masses))
    moves = [pltpu.make_async_copy(a, b, arrived.at[k]) for k, (a, b) in enumerate(pairs)]
    for move in moves:
        move.start()
    for move in moves:
        move.wait()
    places, speeds = by_node(positions), by_node(velocities)
    moved = [slice_length * (w[0] * speeds[0] + w[1] * speeds[1] + w[2] * speeds[2]) for w in lobatto_weights]
    first = places[0] + moved[0]
    packed = jnp.concatenate([*places, first, masses[...]], axis=0)
    for k in range(ring_z):
        out[k] = packed
    known[0] = speeds[0]
    known[1] = first - half_step * speeds[1] + moved[1]
    known[2] = places[0] + slice_length * speeds[0]


def spread_kernel(far, out):
    for row in range(rows_sent):
        line_of = jnp.concatenate([far[z, row : row + 1] for z in range(ring_z)], axis=0)
        for k in range(ring_y * cores):
            out[k, row] = line_of


def nodes_of(mine, count):
    return [mine[3 * n : 3 * n + 3] for n in range(count)]


def rows_of(packed, near, far, first):
    places = [packed[near, first + c, far : far + 1] for c in range(3)]
    return jnp.concatenate(places, axis=0), packed[near, 12, far : far + 1]


def near_block(here, block):
    return (here[0] + block + 1) % (ring_y * cores)


def column_kernel(far, own, total):
    def read(node, block, z):
        return far[z, 3 * node : 3 * node + 3], far[z, 12:13]

    total[...] = jnp.zeros_like(total)
    add_pulls(nodes_of(own[0], 4), read, 1, total)


def old_kernel(here, packed, own, known, column, out, state, total):
    def read(node, block, far):
        near = near_block(here, block)
        return rows_of(packed, near, far, 3 * node)

    total[...] = column[0:3]
    owns = nodes_of(own[0], 3)
    add_pulls(owns, read, ring_y * cores - 1, total)
    old = forces(owns, total)
    kicks = [slice_length * (w[0] * old[0] + w[1] * old[1] + w[2] * old[2]) for w in lobatto_weights]
    first_speed = known[0] + kicks[0]
    second = known[1] + half_step * first_speed
    halves = [second[:, :128], second[:, 128:]]
    for c in range(3):
        row = jnp.concatenate([half[c : c + 1] for half in halves], axis=0)
        for k in range(sources):
            out[k, c] = row
    state[0] = first_speed
    state[1] = first_speed - half_step * old[1] + kicks[1]
    state[2] = second
    state[3] = second - known[2]


def middle_kernel(here, now, packed, own, known, state, column, places, speeds, drift, total):
    def read(node, block, far):
        near = near_block(here, block)
        return rows_of(packed, near, far, 9)

    mine = own[0]
    total[...] = column[3:4]
    owns = [mine[9:12]]
    add_pulls(owns, read, ring_y * cores - 1, total)
    (force,) = forces(owns, total)
    last = state[1] + half_step * force
    for c in range(3):
        places[0, c] = jnp.concatenate([mine[9 + c : 10 + c], state[2, c : c + 1]], axis=0)
        speeds[0, c] = jnp.concatenate([state[0, c : c + 1], last[c : c + 1]], axis=0)
    kick = last - known[0]
    drift[0:3] = state[3] - (slice_length * now[0].astype(f32)) * kick
    drift[3:6] = kick


def line_kernel(now, drift, *others_and_out):
    *others, out = others_and_out
    x = now[0] // line
    mine = drift[...]
    passed = jnp.zeros_like(mine)
    for k, other in enumerate(others):
        passed = passed + other[...] * jnp.where((x ^ (k + 1)) < x, 1.0, 0.0)
    for k in range(line):
        out[k, 0:6] = passed
        out[k, 6:12] = mine


def end_kernel(packed, places, state, out, total):
    def read(node, near, far):
        source = (near // cores) * (ring_z * cores) + far * cores + near % cores
        halves = [jnp.concatenate([places[source, c, h : h + 1] for c in range(3)], axis=0) for h in range(2)]
        return jnp.concatenate(halves, axis=1), packed[near, 12, far : far + 1]

    (force,) = pulls([state[2]], read, total)
    for c in range(3):
        out[c] = force[c : c + 1]


def start_kernel(here, drift, places, speeds, start_places, start_speeds):
    now = here[0].astype(f32)
    mine = here[0] % line
    passed = jnp.zeros((6, drift.shape[2]), f32)
    for k in range(line):
        passed = passed + drift[k, 0:6] + drift[k, 6:12] * jnp.where(k < mine, 1.0, 0.0)
    kick = passed[3:6]
    place = places[...] + (slice_length * now) * speeds[...] + passed[0:3] + (slice_length * (now - 1.0)) * kick
    speed = speeds[...] + kick
    for c in range(3):
        start_places[c] = place[c : c + 1]
        start_speeds[c] = speed[c : c + 1]


def run(kernel, outs, places=(), scratch=(), flops=0, room=40):
    cost = pl.CostEstimate(flops=flops, bytes_accessed=0, transcendentals=0) if flops else None

    def call(*args):
        specs = [pl.BlockSpec(memory_space=place) for place in places]
        specs += [pl.BlockSpec(memory_space=pltpu.VMEM)] * (len(args) - len(specs))
        return pl.pallas_call(
            kernel,
            in_specs=specs,
            out_shape=outs,
            scratch_shapes=list(scratch),
            cost_estimate=cost,
            compiler_params=pltpu.CompilerParams(vmem_limit_bytes=room * 2**20),
        )(*args)

    return call


def sums(nodes):
    return (pltpu.VMEM((nodes, 16, 256), f32),)


def shape(*lengths):
    return jax.ShapeDtypeStruct(lengths, f32)


def body(positions, velocities, masses, initial_places, initial_speeds):
    positions = positions.transpose(1, 2, 0, 3)
    velocities = velocities.transpose(1, 2, 0, 3)
    masses = masses[None]
    landing = [pltpu.VMEM(a.shape, f32) for a in (positions, velocities, masses)]
    own, known = run(
        pack_kernel,
        (shape(ring_z, rows_sent, 256), shape(3, 3, 256)),
        places=(pltpu.HBM,) * 3,
        scratch=(*landing, pltpu.SemaphoreType.DMA((3,))),
        room=60,
    )(positions, velocities, masses)
    far = lax.all_to_all(own, "space", 0, 0, axis_index_groups=far_groups(), tiled=True)
    near = run(spread_kernel, shape(ring_y * cores, rows_sent, ring_z, 256))(far)
    packed = lax.all_to_all(near, "space", 0, 0, axis_index_groups=near_groups(), tiled=True)
    column = run(column_kernel, shape(4, 16, 256), flops=pull_flops)(far, own)
    place = lax.axis_index("space").astype(jnp.int32)
    place = ((place // (ring_z * cores)) * cores + place % cores)[None]
    second, state = run(
        old_kernel, (shape(sources, 3, 2, 128), shape(4, 3, 256)), places=(pltpu.SMEM,), scratch=sums(3)
    )(place, packed, own, known, column)
    gathered = lax.all_to_all(second, "space", 0, 0, tiled=True)
    now = lax.axis_index("tm").astype(jnp.int32)[None]
    node_places, node_speeds, drift = run(
        middle_kernel,
        (shape(1, 3, 2, 256), shape(1, 3, 2, 256), shape(6, 256)),
        places=(pltpu.SMEM, pltpu.SMEM),
        scratch=sums(1),
        flops=pull_flops,
    )(place, now, packed, own, known, state, column)
    others = [
        lax.ppermute(drift, "tm", [(t, t ^ (k * line)) for t in range(slices)]) for k in range(1, slices // line)
    ]
    drift = run(line_kernel, shape(line, 12, 256), places=(pltpu.SMEM,))(now, drift, *others)
    drift, gathered = lax.optimization_barrier((drift, gathered))
    drift = lax.all_to_all(drift, "tm", 0, 0, axis_index_groups=line_groups(), tiled=True)
    end_force = run(end_kernel, shape(3, 1, 256), scratch=sums(1), flops=pull_flops)(packed, gathered, state)
    start_places, start_speeds = run(start_kernel, (shape(3, 1, 256), shape(3, 1, 256)), places=(pltpu.SMEM,))(
        now, drift, initial_places, initial_speeds
    )
    return (
        node_places.transpose(0, 2, 1, 3),
        node_speeds.transpose(0, 2, 1, 3),
        end_force.transpose(1, 0, 2),
        start_places.transpose(1, 0, 2),
        start_speeds.transpose(1, 0, 2),
    )


def solution(mesh):
    return jax.shard_map(
        body,
        mesh=mesh,
        in_specs=(
            P("tm", None, None, "space"),
            P("tm", None, None, "space"),
            P("space"),
            P(None, "space"),
            P(None, "space"),
        ),
        out_specs=(
            P("tm", None, None, "space"),
            P("tm", None, None, "space"),
            P("tm", None, "space"),
            P("tm", None, "space"),
            P("tm", None, "space"),
        ),
        check_vma=False,
    )
```

```python
import jax
import jax.numpy as jnp
import numpy as np
from jax import lax
from jax.experimental import pallas as pl
from jax.experimental.pallas import tpu as pltpu
from jax.sharding import PartitionSpec as P

soften = 0.01
slice_length = 0.25
half_step = 0.5 * slice_length
lobatto_weights = ((5.0 / 24.0, 1.0 / 3.0, -1.0 / 24.0), (-1.0 / 24.0, 1.0 / 3.0, 5.0 / 24.0))

bodies = 8192
sources = 32
slices = 16
ring_y, ring_z, cores = 4, 4, 2
column = ring_z * cores
line = 4
rows_sent = 13
f32 = jnp.float32
bf16 = jnp.bfloat16
pull_flops = 2 * 256 * bodies * 256 * 3


def far_groups():
    return [[y * column + k for k in range(column)] for y in range(ring_y)]


def near_groups():
    return [[y * column + k for y in range(ring_y)] for k in range(column)]


def line_groups():
    return [[x * line + k for k in range(line)] for x in range(slices // line)]


def product(a, b, contract):
    return lax.dot_general(a, b, (contract, ((), ())), preferred_element_type=f32)


def in_three(a):
    high = a.astype(bf16).astype(f32)
    rest = a - high
    middle = rest.astype(bf16).astype(f32)
    low = (rest - middle).astype(bf16).astype(f32)
    return high, middle, low


def own_rows(places):
    squares = jnp.sum(places * places, axis=0, keepdims=True) + soften
    high, middle, low = in_three(-2.0 * places)
    one, zero = jnp.ones_like(squares), jnp.zeros_like(squares)
    return jnp.concatenate(
        [high, high, high, middle, middle, middle, low, low, *in_three(squares), one, one, one, zero, zero], axis=0
    ).astype(bf16)


def far_rows(places):
    squares = jnp.sum(places * places, axis=0, keepdims=True)
    high, middle, low = in_three(places)
    one, zero = jnp.ones_like(squares), jnp.zeros_like(squares)
    return jnp.concatenate(
        [high, middle, low, high, middle, low, high, middle, one, one, one, *in_three(squares), zero, zero], axis=0
    ).astype(bf16)


def weight_rows(places, mass):
    weights = jnp.concatenate([places * mass, mass], axis=0)
    return jnp.concatenate([*in_three(weights), jnp.zeros_like(weights)], axis=0).astype(bf16)


def pull_from(source, own, weight):
    inverse = lax.rsqrt(product(source, own, ((0,), (0,))))
    kernel = inverse * inverse * inverse
    high = kernel.astype(bf16)
    low = (kernel - high.astype(f32)).astype(bf16)
    return product(weight, high, ((1,), (0,))) + product(weight, low, ((1,), (0,)))


def add_pulls(owns, read, blocks, total):
    rows = [own_rows(own) for own in owns]

    def one(block, carry):
        for far in range(column):
            for node in range(len(owns)):
                places, mass = read(node, block, far)
                total[node] += pull_from(far_rows(places), rows[node], weight_rows(places, mass))
        return carry

    lax.fori_loop(0, blocks, one, 0, unroll=blocks)


def forces(owns, total):
    found = []
    for node, own in enumerate(owns):
        sums = total[node]
        sums = sums[0:4] + sums[4:8] + sums[8:12]
        found.append((sums[0:3] - own * sums[3:4]) * (1.0 / bodies))
    return found


def pulls(owns, read, total):
    total[...] = jnp.zeros_like(total)
    add_pulls(owns, read, ring_y, total)
    return forces(owns, total)


def by_node(array):
    return [jnp.concatenate([array[node, c] for c in range(3)], axis=0) for node in range(3)]


def pack_kernel(positions_in, velocities_in, masses_in, out, known, positions, velocities, masses, arrived):
    pairs = ((positions_in, positions), (velocities_in, velocities), (masses_in, masses))
    moves = [pltpu.make_async_copy(a, b, arrived.at[k]) for k, (a, b) in enumerate(pairs)]
    for move in moves:
        move.start()
    for move in moves:
        move.wait()
    places, speeds = by_node(positions), by_node(velocities)
    moved = [slice_length * (w[0] * speeds[0] + w[1] * speeds[1] + w[2] * speeds[2]) for w in lobatto_weights]
    first = places[0] + moved[0]
    packed = jnp.concatenate([*places, first, masses[...]], axis=0)
    for k in range(column):
        out[k] = packed
    known[0] = speeds[0]
    known[1] = first - half_step * speeds[1] + moved[1]
    known[2] = places[0] + slice_length * speeds[0]


def spread_kernel(far, out):
    for row in range(rows_sent):
        line_of = jnp.concatenate([far[z, row : row + 1] for z in range(column)], axis=0)
        for k in range(ring_y):
            out[k, row] = line_of


def nodes_of(mine, count):
    return [mine[3 * n : 3 * n + 3] for n in range(count)]


def rows_of(packed, near, far, first):
    places = [packed[near, first + c, far : far + 1] for c in range(3)]
    return jnp.concatenate(places, axis=0), packed[near, 12, far : far + 1]


def near_block(here, block):
    return (here[0] + block + 1) % ring_y


def column_kernel(far, own, total):
    def read(node, block, z):
        return far[z, 3 * node : 3 * node + 3], far[z, 12:13]

    total[...] = jnp.zeros_like(total)
    add_pulls(nodes_of(own[0], 4), read, 1, total)


def old_kernel(here, packed, own, known, begun, out, state, total):
    def read(node, block, far):
        near = near_block(here, block)
        return rows_of(packed, near, far, 3 * node)

    total[...] = begun[0:3]
    owns = nodes_of(own[0], 3)
    add_pulls(owns, read, ring_y - 1, total)
    old = forces(owns, total)
    kicks = [slice_length * (w[0] * old[0] + w[1] * old[1] + w[2] * old[2]) for w in lobatto_weights]
    first_speed = known[0] + kicks[0]
    second = known[1] + half_step * first_speed
    halves = [second[:, :128], second[:, 128:]]
    for c in range(3):
        row = jnp.concatenate([half[c : c + 1] for half in halves], axis=0)
        for k in range(sources):
            out[k, c] = row
    state[0] = first_speed
    state[1] = first_speed - half_step * old[1] + kicks[1]
    state[2] = second
    state[3] = second - known[2]


def middle_kernel(here, now, packed, own, known, state, begun, places, speeds, drift, total):
    def read(node, block, far):
        near = near_block(here, block)
        return rows_of(packed, near, far, 9)

    mine = own[0]
    total[...] = begun[3:4]
    owns = [mine[9:12]]
    add_pulls(owns, read, ring_y - 1, total)
    (force,) = forces(owns, total)
    last = state[1] + half_step * force
    for c in range(3):
        places[0, c] = jnp.concatenate([mine[9 + c : 10 + c], state[2, c : c + 1]], axis=0)
        speeds[0, c] = jnp.concatenate([state[0, c : c + 1], last[c : c + 1]], axis=0)
    kick = last - known[0]
    drift[0:3] = state[3] - (slice_length * now[0].astype(f32)) * kick
    drift[3:6] = kick


def line_kernel(now, drift, *others_and_out):
    *others, out = others_and_out
    x = now[0] // line
    mine = drift[...]
    passed = jnp.zeros_like(mine)
    for k, other in enumerate(others):
        passed = passed + other[...] * jnp.where((x ^ (k + 1)) < x, 1.0, 0.0)
    for k in range(line):
        out[k, 0:6] = passed
        out[k, 6:12] = mine


def end_kernel(packed, places, state, out, total):
    def read(node, near, far):
        source = near * column + far
        halves = [jnp.concatenate([places[source, c, h : h + 1] for c in range(3)], axis=0) for h in range(2)]
        return jnp.concatenate(halves, axis=1), packed[near, 12, far : far + 1]

    (force,) = pulls([state[2]], read, total)
    for c in range(3):
        out[c] = force[c : c + 1]


def start_kernel(here, drift, places, speeds, start_places, start_speeds):
    now = here[0].astype(f32)
    mine = here[0] % line
    passed = jnp.zeros((6, drift.shape[2]), f32)
    for k in range(line):
        passed = passed + drift[k, 0:6] + drift[k, 6:12] * jnp.where(k < mine, 1.0, 0.0)
    kick = passed[3:6]
    place = places[...] + (slice_length * now) * speeds[...] + passed[0:3] + (slice_length * (now - 1.0)) * kick
    speed = speeds[...] + kick
    for c in range(3):
        start_places[c] = place[c : c + 1]
        start_speeds[c] = speed[c : c + 1]


def run(kernel, outs, places=(), scratch=(), flops=0, room=40):
    cost = pl.CostEstimate(flops=flops, bytes_accessed=0, transcendentals=0) if flops else None

    def call(*args):
        specs = [pl.BlockSpec(memory_space=place) for place in places]
        specs += [pl.BlockSpec(memory_space=pltpu.VMEM)] * (len(args) - len(specs))
        return pl.pallas_call(
            kernel,
            in_specs=specs,
            out_shape=outs,
            scratch_shapes=list(scratch),
            cost_estimate=cost,
            compiler_params=pltpu.CompilerParams(vmem_limit_bytes=room * 2**20),
        )(*args)

    return call


def sums(nodes):
    return (pltpu.VMEM((nodes, 16, 256), f32),)


def shape(*lengths):
    return jax.ShapeDtypeStruct(lengths, f32)


def body(positions, velocities, masses, initial_places, initial_speeds):
    positions = positions.transpose(1, 2, 0, 3)
    velocities = velocities.transpose(1, 2, 0, 3)
    masses = masses[None]
    landing = [pltpu.VMEM(a.shape, f32) for a in (positions, velocities, masses)]
    own, known = run(
        pack_kernel,
        (shape(column, rows_sent, 256), shape(3, 3, 256)),
        places=(pltpu.HBM,) * 3,
        scratch=(*landing, pltpu.SemaphoreType.DMA((3,))),
        room=60,
    )(positions, velocities, masses)
    far = lax.all_to_all(own, "space", 0, 0, axis_index_groups=far_groups(), tiled=True)
    near = run(spread_kernel, shape(ring_y, rows_sent, column, 256))(far)
    packed = lax.all_to_all(near, "space", 0, 0, axis_index_groups=near_groups(), tiled=True)
    begun = run(column_kernel, shape(4, 16, 256), flops=pull_flops)(far, own)
    place = (lax.axis_index("space").astype(jnp.int32) // column)[None]
    second, state = run(
        old_kernel, (shape(sources, 3, 2, 128), shape(4, 3, 256)), places=(pltpu.SMEM,), scratch=sums(3)
    )(place, packed, own, known, begun)
    gathered = lax.all_to_all(second, "space", 0, 0, tiled=True)
    now = lax.axis_index("tm").astype(jnp.int32)[None]
    node_places, node_speeds, drift = run(
        middle_kernel,
        (shape(1, 3, 2, 256), shape(1, 3, 2, 256), shape(6, 256)),
        places=(pltpu.SMEM, pltpu.SMEM),
        scratch=sums(1),
        flops=pull_flops,
    )(place, now, packed, own, known, state, begun)
    others = [
        lax.ppermute(drift, "tm", [(t, t ^ (k * line)) for t in range(slices)]) for k in range(1, slices // line)
    ]
    drift = run(line_kernel, shape(line, 12, 256), places=(pltpu.SMEM,))(now, drift, *others)
    drift, gathered = lax.optimization_barrier((drift, gathered))
    drift = lax.all_to_all(drift, "tm", 0, 0, axis_index_groups=line_groups(), tiled=True)
    end_force = run(end_kernel, shape(3, 1, 256), scratch=sums(1), flops=pull_flops)(packed, gathered, state)
    start_places, start_speeds = run(start_kernel, (shape(3, 1, 256), shape(3, 1, 256)), places=(pltpu.SMEM,))(
        now, drift, initial_places, initial_speeds
    )
    return (
        node_places.transpose(0, 2, 1, 3),
        node_speeds.transpose(0, 2, 1, 3),
        end_force.transpose(1, 0, 2),
        start_places.transpose(1, 0, 2),
        start_speeds.transpose(1, 0, 2),
    )


def solution(mesh):
    return jax.shard_map(
        body,
        mesh=mesh,
        in_specs=(
            P("tm", None, None, "space"),
            P("tm", None, None, "space"),
            P("space"),
            P(None, "space"),
            P(None, "space"),
        ),
        out_specs=(
            P("tm", None, None, "space"),
            P("tm", None, None, "space"),
            P("tm", None, "space"),
            P("tm", None, "space"),
            P("tm", None, "space"),
        ),
        check_vma=False,
    )
```

```python
import jax
import jax.numpy as jnp
import numpy as np
from jax import lax
from jax.experimental import pallas as pl
from jax.experimental.pallas import tpu as pltpu
from jax.sharding import PartitionSpec as P

soften = 0.01
slice_length = 0.25
half_step = 0.5 * slice_length
lobatto_weights = ((5.0 / 24.0, 1.0 / 3.0, -1.0 / 24.0), (-1.0 / 24.0, 1.0 / 3.0, 5.0 / 24.0))

bodies = 8192
sources = 32
slices = 16
ring_y, ring_z, cores = 4, 4, 2
line = 4
rows_sent = 13
f32 = jnp.float32
bf16 = jnp.bfloat16
pull_flops = 2 * 256 * bodies * 256 * 3


def far_groups():
    places = np.arange(sources).reshape(ring_y, ring_z, cores)
    return [[int(p) for p in places[y, :, c]] for y in range(ring_y) for c in range(cores)]


def near_groups():
    places = np.arange(sources).reshape(ring_y, ring_z, cores)
    return [[int(p) for p in places[:, z, :].reshape(-1)] for z in range(ring_z)]


def line_groups():
    return [[x * line + k for k in range(line)] for x in range(slices // line)]


def product(a, b, contract):
    return lax.dot_general(a, b, (contract, ((), ())), preferred_element_type=f32)


def in_three(a):
    high = a.astype(bf16).astype(f32)
    rest = a - high
    middle = rest.astype(bf16).astype(f32)
    low = (rest - middle).astype(bf16).astype(f32)
    return high, middle, low


def own_rows(places):
    squares = jnp.sum(places * places, axis=0, keepdims=True) + soften
    high, middle, low = in_three(-2.0 * places)
    one, zero = jnp.ones_like(squares), jnp.zeros_like(squares)
    return jnp.concatenate(
        [high, high, high, middle, middle, middle, low, low, *in_three(squares), one, one, one, zero, zero], axis=0
    ).astype(bf16)


def far_rows(places):
    squares = jnp.sum(places * places, axis=0, keepdims=True)
    high, middle, low = in_three(places)
    one, zero = jnp.ones_like(squares), jnp.zeros_like(squares)
    return jnp.concatenate(
        [high, middle, low, high, middle, low, high, middle, one, one, one, *in_three(squares), zero, zero], axis=0
    ).astype(bf16)


def weight_rows(places, mass):
    weights = jnp.concatenate([places * mass, mass], axis=0)
    return jnp.concatenate([*in_three(weights), jnp.zeros_like(weights)], axis=0).astype(bf16)


def pull_from(source, own, weight):
    inverse = lax.rsqrt(product(source, own, ((0,), (0,))))
    kernel = inverse * inverse * inverse
    high = kernel.astype(bf16)
    low = (kernel - high.astype(f32)).astype(bf16)
    return product(weight, high, ((1,), (0,))) + product(weight, low, ((1,), (0,)))


def add_pulls(owns, read, blocks, total):
    rows = [own_rows(own) for own in owns]

    def one(block, carry):
        for far in range(ring_z):
            for node in range(len(owns)):
                places, mass = read(node, block, far)
                total[node] += pull_from(far_rows(places), rows[node], weight_rows(places, mass))
        return carry

    lax.fori_loop(0, blocks, one, 0, unroll=blocks)


def forces(owns, total):
    found = []
    for node, own in enumerate(owns):
        sums = total[node]
        sums = sums[0:4] + sums[4:8] + sums[8:12]
        found.append((sums[0:3] - own * sums[3:4]) * (1.0 / bodies))
    return found


def pulls(owns, read, total):
    total[...] = jnp.zeros_like(total)
    add_pulls(owns, read, ring_y * cores, total)
    return forces(owns, total)


def by_node(array):
    return [jnp.concatenate([array[node, c] for c in range(3)], axis=0) for node in range(3)]


def pack_kernel(positions_in, velocities_in, masses_in, out, known, positions, velocities, masses, arrived):
    pairs = ((positions_in, positions), (velocities_in, velocities), (masses_in, masses))
    moves = [pltpu.make_async_copy(a, b, arrived.at[k]) for k, (a, b) in enumerate(pairs)]
    for move in moves:
        move.start()
    for move in moves:
        move.wait()
    places, speeds = by_node(positions), by_node(velocities)
    moved = [slice_length * (w[0] * speeds[0] + w[1] * speeds[1] + w[2] * speeds[2]) for w in lobatto_weights]
    first = places[0] + moved[0]
    packed = jnp.concatenate([*places, first, masses[...]], axis=0)
    for k in range(ring_z):
        out[k] = packed
    known[0] = speeds[0]
    known[1] = first - half_step * speeds[1] + moved[1]
    known[2] = places[0] + slice_length * speeds[0]


def spread_kernel(far, out, once, sent):
    for row in range(rows_sent):
        once[row] = jnp.concatenate([far[z, row : row + 1] for z in range(ring_z)], axis=0)
    moves = [pltpu.make_async_copy(once, out.at[k], sent.at[k]) for k in range(ring_y * cores)]
    for move in moves:
        move.start()
    for move in moves:
        move.wait()


def nodes_of(mine, count):
    return [mine[3 * n : 3 * n + 3] for n in range(count)]


def rows_of(packed, near, far, first):
    places = [packed[near, first + c, far : far + 1] for c in range(3)]
    return jnp.concatenate(places, axis=0), packed[near, 12, far : far + 1]


def near_block(here, block):
    return (here[0] + block + 1) % (ring_y * cores)


def column_kernel(far, own, total):
    def read(node, block, z):
        return far[z, 3 * node : 3 * node + 3], far[z, 12:13]

    total[...] = jnp.zeros_like(total)
    add_pulls(nodes_of(own[0], 4), read, 1, total)


def old_kernel(here, packed, own, known, column, out, state, total):
    def read(node, block, far):
        near = near_block(here, block)
        return rows_of(packed, near, far, 3 * node)

    total[...] = column[0:3]
    owns = nodes_of(own[0], 3)
    add_pulls(owns, read, ring_y * cores - 1, total)
    old = forces(owns, total)
    kicks = [slice_length * (w[0] * old[0] + w[1] * old[1] + w[2] * old[2]) for w in lobatto_weights]
    first_speed = known[0] + kicks[0]
    second = known[1] + half_step * first_speed
    halves = [second[:, :128], second[:, 128:]]
    for c in range(3):
        row = jnp.concatenate([half[c : c + 1] for half in halves], axis=0)
        for k in range(sources):
            out[k, c] = row
    state[0] = first_speed
    state[1] = first_speed - half_step * old[1] + kicks[1]
    state[2] = second
    state[3] = second - known[2]


def middle_kernel(here, now, packed, own, known, state, column, places, speeds, drift, total):
    def read(node, block, far):
        near = near_block(here, block)
        return rows_of(packed, near, far, 9)

    mine = own[0]
    total[...] = column[3:4]
    owns = [mine[9:12]]
    add_pulls(owns, read, ring_y * cores - 1, total)
    (force,) = forces(owns, total)
    last = state[1] + half_step * force
    for c in range(3):
        places[0, c] = jnp.concatenate([mine[9 + c : 10 + c], state[2, c : c + 1]], axis=0)
        speeds[0, c] = jnp.concatenate([state[0, c : c + 1], last[c : c + 1]], axis=0)
    kick = last - known[0]
    drift[0:3] = state[3] - (slice_length * now[0].astype(f32)) * kick
    drift[3:6] = kick


def line_kernel(now, drift, *others_and_out):
    *others, out = others_and_out
    x = now[0] // line
    mine = drift[...]
    passed = jnp.zeros_like(mine)
    for k, other in enumerate(others):
        passed = passed + other[...] * jnp.where((x ^ (k + 1)) < x, 1.0, 0.0)
    for k in range(line):
        out[k, 0:6] = passed
        out[k, 6:12] = mine


def end_kernel(packed, places, state, out, total):
    def read(node, near, far):
        source = (near // cores) * (ring_z * cores) + far * cores + near % cores
        halves = [jnp.concatenate([places[source, c, h : h + 1] for c in range(3)], axis=0) for h in range(2)]
        return jnp.concatenate(halves, axis=1), packed[near, 12, far : far + 1]

    (force,) = pulls([state[2]], read, total)
    for c in range(3):
        out[c] = force[c : c + 1]


def start_kernel(here, drift, places, speeds, start_places, start_speeds):
    now = here[0].astype(f32)
    mine = here[0] % line
    passed = jnp.zeros((6, drift.shape[2]), f32)
    for k in range(line):
        passed = passed + drift[k, 0:6] + drift[k, 6:12] * jnp.where(k < mine, 1.0, 0.0)
    kick = passed[3:6]
    place = places[...] + (slice_length * now) * speeds[...] + passed[0:3] + (slice_length * (now - 1.0)) * kick
    speed = speeds[...] + kick
    for c in range(3):
        start_places[c] = place[c : c + 1]
        start_speeds[c] = speed[c : c + 1]


def run(kernel, outs, places=(), scratch=(), flops=0, room=40, out_place=None):
    cost = pl.CostEstimate(flops=flops, bytes_accessed=0, transcendentals=0) if flops else None

    def call(*args):
        specs = [pl.BlockSpec(memory_space=place) for place in places]
        specs += [pl.BlockSpec(memory_space=pltpu.VMEM)] * (len(args) - len(specs))
        return pl.pallas_call(
            kernel,
            in_specs=specs,
            out_shape=outs,
            **({"out_specs": pl.BlockSpec(memory_space=out_place)} if out_place else {}),
            scratch_shapes=list(scratch),
            cost_estimate=cost,
            compiler_params=pltpu.CompilerParams(vmem_limit_bytes=room * 2**20),
        )(*args)

    return call


def sums(nodes):
    return (pltpu.VMEM((nodes, 16, 256), f32),)


def shape(*lengths):
    return jax.ShapeDtypeStruct(lengths, f32)


def body(positions, velocities, masses, initial_places, initial_speeds):
    positions = positions.transpose(1, 2, 0, 3)
    velocities = velocities.transpose(1, 2, 0, 3)
    masses = masses[None]
    landing = [pltpu.VMEM(a.shape, f32) for a in (positions, velocities, masses)]
    own, known = run(
        pack_kernel,
        (shape(ring_z, rows_sent, 256), shape(3, 3, 256)),
        places=(pltpu.HBM,) * 3,
        scratch=(*landing, pltpu.SemaphoreType.DMA((3,))),
        room=60,
    )(positions, velocities, masses)
    far = lax.all_to_all(own, "space", 0, 0, axis_index_groups=far_groups(), tiled=True)
    near = run(
        spread_kernel,
        shape(ring_y * cores, rows_sent, ring_z, 256),
        scratch=(pltpu.VMEM((rows_sent, ring_z, 256), f32), pltpu.SemaphoreType.DMA((ring_y * cores,))),
        out_place=pltpu.HBM,
    )(far)
    packed = lax.all_to_all(near, "space", 0, 0, axis_index_groups=near_groups(), tiled=True)
    column = run(column_kernel, shape(4, 16, 256), flops=pull_flops)(far, own)
    place = lax.axis_index("space").astype(jnp.int32)
    place = ((place // (ring_z * cores)) * cores + place % cores)[None]
    second, state = run(
        old_kernel, (shape(sources, 3, 2, 128), shape(4, 3, 256)), places=(pltpu.SMEM,), scratch=sums(3)
    )(place, packed, own, known, column)
    gathered = lax.all_to_all(second, "space", 0, 0, tiled=True)
    now = lax.axis_index("tm").astype(jnp.int32)[None]
    node_places, node_speeds, drift = run(
        middle_kernel,
        (shape(1, 3, 2, 256), shape(1, 3, 2, 256), shape(6, 256)),
        places=(pltpu.SMEM, pltpu.SMEM),
        scratch=sums(1),
        flops=pull_flops,
    )(place, now, packed, own, known, state, column)
    others = [
        lax.ppermute(drift, "tm", [(t, t ^ (k * line)) for t in range(slices)]) for k in range(1, slices // line)
    ]
    drift = run(line_kernel, shape(line, 12, 256), places=(pltpu.SMEM,))(now, drift, *others)
    drift, gathered = lax.optimization_barrier((drift, gathered))
    drift = lax.all_to_all(drift, "tm", 0, 0, axis_index_groups=line_groups(), tiled=True)
    end_force = run(end_kernel, shape(3, 1, 256), scratch=sums(1), flops=pull_flops)(packed, gathered, state)
    start_places, start_speeds = run(start_kernel, (shape(3, 1, 256), shape(3, 1, 256)), places=(pltpu.SMEM,))(
        now, drift, initial_places, initial_speeds
    )
    return (
        node_places.transpose(0, 2, 1, 3),
        node_speeds.transpose(0, 2, 1, 3),
        end_force.transpose(1, 0, 2),
        start_places.transpose(1, 0, 2),
        start_speeds.transpose(1, 0, 2),
    )


def solution(mesh):
    return jax.shard_map(
        body,
        mesh=mesh,
        in_specs=(
            P("tm", None, None, "space"),
            P("tm", None, None, "space"),
            P("space"),
            P(None, "space"),
            P(None, "space"),
        ),
        out_specs=(
            P("tm", None, None, "space"),
            P("tm", None, None, "space"),
            P("tm", None, "space"),
            P("tm", None, "space"),
            P("tm", None, "space"),
        ),
        check_vma=False,
    )
```
